128 devices in a mesh: dp: 8 (over z, core), tensor: 16 (over x, y).
Axes of the slice: x: 4, y: 4, z: 4, core: 2. Of those that a mesh axis runs over, the one named last changes fastest.
Arguments:
- activations: bfloat16 [8, 1024, 5120], P('dp'), may hold values from -6 to 6
- out_grad_q: bfloat16 [8, 1024, 5120], P('dp', None, 'tensor'), may hold values from -0.1875 to 0.1875
- out_grad_kv: bfloat16 [8, 1024, 2048], P('dp', None, 'tensor'), may hold values from -0.1875 to 0.1875
- error_q: bfloat16 [8, 5120, 5120], P('dp', None, 'tensor'), may hold values from -4 to 4
- error_kv: bfloat16 [8, 5120, 2048], P('dp', None, 'tensor'), may hold values from -4 to 4
- basis_q: float32 [5120, 32], P('tensor'), may hold values from -0.078125 to 0.078125
- basis_kv: float32 [2048, 32], P('tensor'), may hold values from -0.125 to 0.125
Outputs:
- update_q: bfloat16 [5120, 5120], P(None, 'tensor')
- update_kv: bfloat16 [5120, 2048], P(None, 'tensor')
- error_q_next: bfloat16 [8, 5120, 5120], P('dp', None, 'tensor')
- error_kv_next: bfloat16 [8, 5120, 2048], P('dp', None, 'tensor')
- basis_q_next: float32 [5120, 32], P('tensor')
- basis_kv_next: float32 [2048, 32], P('tensor')
The draws below stay inside these ranges and needn't reach their ends.
All inputs are finite; a program needn't handle non-finite values.
Results may differ from the reference program's by a relative error of at most 0.0012.
Values sent between devices are 32-bit elements; how exact they have to be, the bound alone decides.
A program may use at most 128 MiB of HBM per device.

```python
import jax
import jax.numpy as jnp
from jax import lax

D = 5120
COLS_Q = 5120
COLS_KV = 2048
RANK = 32
TOK_DEV = 1024
REPLICAS = 8


def steps_of(key, extent, cuts, least, top_value):
    def one(dim, parts):
        draws = jax.random.uniform(jax.random.fold_in(jax.random.fold_in(key, 6), dim), (parts,), jnp.float32, least / len(cuts), top_value / len(cuts))
        return jnp.repeat(jnp.exp(draws), extent[dim] // parts).reshape((-1,) + (1,) * (len(extent) - dim - 1))

    gain = one(*cuts[0])
    for cut in cuts[1:]:
        gain = gain * one(*cut)
    return gain


def gaussian(stream_key, shape, deviation, reach, shards=(), held_as=jnp.bfloat16):
    result = deviation * jax.random.normal(stream_key, shape, jnp.float32)
    if shards:
        result = result * steps_of(stream_key, shape, shards, -0.22, 0.18)
    return jnp.clip(result, -reach, reach).astype(held_as)


def setup_inputs(seed: int = 0) -> dict:
    arg_keys = jax.random.split(jax.random.key(seed), 8)
    return {
        "activations": gaussian(arg_keys[0], (REPLICAS, TOK_DEV, D), 1.0, 6.0, ((0, 8),)),
        "out_grad_q": gaussian(arg_keys[1], (REPLICAS, TOK_DEV, COLS_Q), TOK_DEV ** -0.5, 0.1875, ((0, 8), (2, 16))),
        "out_grad_kv": gaussian(arg_keys[2], (REPLICAS, TOK_DEV, COLS_KV), TOK_DEV ** -0.5, 0.1875, ((0, 8), (2, 16))),
        "error_q": gaussian(arg_keys[3], (REPLICAS, D, COLS_Q), 0.5, 4.0, ((0, 8), (2, 16))),
        "error_kv": gaussian(arg_keys[4], (REPLICAS, D, COLS_KV), 0.5, 4.0, ((0, 8), (2, 16))),
        "basis_q": gaussian(arg_keys[5], (COLS_Q, RANK), COLS_Q ** -0.5, 0.078125, ((0, 16),), jnp.float32),
        "basis_kv": gaussian(arg_keys[6], (COLS_KV, RANK), COLS_KV ** -0.5, 0.125, ((0, 16),), jnp.float32),
    }


def compress(activations, out_grad, error, basis):
    grads = jnp.einsum('rtd,rtc->rdc', activations.astype(jnp.float32), out_grad.astype(jnp.float32), precision=lax.Precision.HIGHEST)
    full = grads + error.astype(jnp.float32)
    left = jnp.einsum('rdc,ck->dk', full, basis, precision=lax.Precision.HIGHEST)
    gram = jnp.dot(left.T, left, precision=lax.Precision.HIGHEST)
    lower = jnp.linalg.cholesky(gram)
    ortho = lax.linalg.triangular_solve(lower, left, left_side=False, lower=True, transpose_a=True)
    basis_next = jnp.einsum('rdc,dk->ck', full, ortho, precision=lax.Precision.HIGHEST) / REPLICAS
    approx = jnp.dot(ortho, basis_next.T, precision=lax.Precision.HIGHEST)
    update = approx.astype(jnp.bfloat16)
    error_next = (full - approx[None]).astype(jnp.bfloat16)
    return (update, error_next, basis_next)

def reference(activations, out_grad_q, out_grad_kv, error_q, error_kv, basis_q, basis_kv):
    update_q, error_q_next, basis_q_next = compress(activations, out_grad_q, error_q, basis_q)
    update_kv, error_kv_next, basis_kv_next = compress(activations, out_grad_kv, error_kv, basis_kv)
    return (update_q, update_kv, error_q_next, error_kv_next, basis_q_next, basis_kv_next)
```

```python
import functools

import jax
import jax.numpy as jnp
from jax import lax
from jax.experimental import pallas as pl
from jax.experimental.pallas import tpu as pltpu
from jax.sharding import PartitionSpec as P

F32 = jnp.float32
BF16 = jnp.bfloat16
MESH = pl.DeviceIdType.MESH
HIGHEST = lax.Precision.HIGHEST
MIB = 1 << 20

SIDE = 4
D = 5120
QUART = D // SIDE
TOK = 1024
CQ, CKV = 320, 128
COLS = CQ + CKV
RANK = 32
WIDE = 512
SUB = 640
ROT = (1, 2, 3, 0)
AG_ORDER = (0, 1, 3, 2)


def mm(a, b):
    return jnp.dot(a, b, preferred_element_type=F32)


def mm_t(a, b, precision=None):
    return lax.dot_general(a, b, (((1,), (1,)), ((), ())), preferred_element_type=F32, precision=precision)


def tmm(a, b, precision=None):
    return lax.dot_general(a, b, (((0,), (0,)), ((), ())), preferred_element_type=F32, precision=precision)


def halves(v):
    high = v.astype(BF16)
    return high, (v - high.astype(F32)).astype(BF16)


def eliminate(a, off):
    row = lax.broadcasted_iota(jnp.int32, (RANK, 128), 0)
    lane = lax.broadcasted_iota(jnp.int32, (RANK, 128), 1)
    for k in range(RANK - 1):
        col = jnp.broadcast_to(a[:, off + k : off + k + 1], (RANK, 128))
        scaled = a[k : k + 1, :] / col[k : k + 1, :]
        a = a - jnp.where(row > k, col, 0.0) * scaled
    diag = jnp.sum(jnp.where(lane == row + off, a, 0.0), axis=1, keepdims=True)
    return a * lax.rsqrt(diag)


def reduce_kernel(
    act, ogq, ogkv, eq, ekv, bq, bkv,
    fqh_o, fqm_o, fkv_o, lq_o, tkv_o, zq_o, zkv_o, bn_o,
    act_v, ogkv_v, og_v, eq_v, ekv_v, bq_v, bkv_v, pst_v, bq2_v, bkv2_v,
    loc_v, xr_v, sum_v, rs_buf, zbuf, lt_v, lst_v, lq_v, tkv_v, fqh_v, fqm_v, fkv_v,
    yloc_v, yx_v, yz_v, ysum_v, gram_v, zq_v, zkv_v, bn_v,
    ld, lda, xs, xr, rs_s, rs_r, zs, zr, ag_s, ag_r, fw_s, fw_r, y_s, y_r, out_s,
):
    dp, t = lax.axis_index("dp"), lax.axis_index("tensor")
    z, c = dp // 2, lax.rem(dp, 2)
    x, y = t // SIDE, lax.rem(t, SIDE)
    partner = (z * 2 + 1 - c, t)

    def plane(dx, dy):
        return (dp, lax.rem(x + dx, SIDE) * SIDE + lax.rem(y + dy, SIDE))

    def along_z(dz):
        return (lax.rem(z + dz, SIDE) * 2 + c, t)

    chunks = [lax.rem(x + dx, SIDE) for dx in ROT]

    first = [
        pltpu.make_async_copy(src, dst, ld.at[i])
        for i, (src, dst) in enumerate(
            [(ogq.at[0], og_v.at[pl.ds(CKV, CQ), :]), (ogkv.at[0], ogkv_v), (bq, bq_v), (bkv, bkv_v)]
        )
    ]
    for cp in first:
        cp.start()
    loads = []
    for k, g in enumerate(chunks):
        at = pl.ds(pl.multiple_of(g * QUART, QUART), QUART)
        cps = [
            pltpu.make_async_copy(act.at[0, :, at], act_v.at[g], lda.at[k, 0]),
            pltpu.make_async_copy(eq.at[0, :, at], eq_v.at[g], lda.at[k, 1]),
            pltpu.make_async_copy(ekv.at[0, at, :], ekv_v.at[g], lda.at[k, 2]),
        ]
        for cp in cps:
            cp.start()
        loads.append(cps)

    barrier = pltpu.get_barrier_semaphore()
    peers = [partner]
    peers += [plane(dx, dy) for dx in range(SIDE) for dy in range(SIDE) if dx or dy]
    peers += [along_z(dz) for dz in (1, 2, 3)]
    for p in peers:
        pl.semaphore_signal(barrier, inc=1, device_id=p, device_id_type=MESH)

    for cp in first:
        cp.wait()
    og_v[:CKV, :] = jnp.transpose(ogkv_v[...])
    for src, b2, og_rows, base in ((bq_v, bq2_v, slice(CKV, COLS), 0), (bkv_v, bkv2_v, slice(0, CKV), 2 * RANK)):
        bt = src[...]
        high, mid = halves(bt)
        low = (bt - high.astype(F32) - mid.astype(F32)).astype(BF16)
        b2[:RANK, :] = high
        b2[RANK:, :] = mid
        og_w = og_v[og_rows, :]
        proj = mm(high, og_w) + (mm(mid, og_w) + mm(low, og_w))
        p_high, p_mid = halves(proj)
        pst_v[base : base + RANK, :] = p_high
        pst_v[base + RANK : base + 2 * RANK, :] = p_mid

    def exchange(k):
        theirs = pl.ds(pl.multiple_of((1 - c) * RANK, RANK), RANK)
        return pltpu.make_async_remote_copy(
            src_ref=loc_v.at[k, theirs, :], dst_ref=xr_v.at[k], send_sem=xs.at[k], recv_sem=xr.at[k],
            device_id=partner, device_id_type=MESH,
        )

    def scatter(k):
        exchange(k).wait()
        mine = pl.ds(pl.multiple_of(c * RANK, RANK), RANK)
        sum_v[k] = loc_v[k, mine, :] + xr_v[k]
        for dy in range(SIDE):
            if ROT[k] or dy:
                rows = pl.ds(pl.multiple_of(lax.rem(y + dy, SIDE) * 8, 8), 8)
                pltpu.make_async_remote_copy(
                    src_ref=sum_v.at[k, rows, :], dst_ref=rs_buf.at[ROT[k] * SIDE + dy - 1],
                    send_sem=rs_s, recv_sem=rs_r,
                    device_id=plane(ROT[k], dy), device_id_type=MESH,
                ).start()

    for k, g in enumerate(chunks):
        for cp in loads[k]:
            cp.wait()
        bq2, bkv2 = bq2_v[...], bkv2_v[...]
        pst = pst_v[...]
        for i in range(QUART // 256):
            cut = slice(i * 256, (i + 1) * 256)
            prod = mm(pst, act_v[g, :, cut])
            from_q = mm(bq2, eq_v[g, :, cut])
            from_kv = mm_t(bkv2, ekv_v[g, cut, :])
            loc_v[k, :RANK, cut] = (prod[:RANK] + prod[RANK : 2 * RANK]) + (from_q[:RANK] + from_q[RANK:])
            loc_v[k, RANK:, cut] = (prod[2 * RANK : 3 * RANK] + prod[3 * RANK :]) + (from_kv[:RANK] + from_kv[RANK:])
        if k == 0:
            pl.semaphore_wait(barrier, len(peers))
        exchange(k).start()
        if k >= 1:
            scatter(k - 1)
    scatter(SIDE - 1)

    def gradient(lo, hi):
        def body(i, _):
            g, j = i // (QUART // SUB), lax.rem(i, QUART // SUB)
            at = pl.ds(pl.multiple_of(j * SUB, SUB), SUB)
            grads = mm(og_v[...], act_v[g, :, at])
            high, mid = halves(jnp.transpose(grads[:CKV]) + ekv_v[g, at, :].astype(F32))
            fkv_v[g, at, :CKV] = high
            fkv_v[g, at, CKV:] = mid
            high, mid = halves(grads[CKV:] + eq_v[g, :, at].astype(F32))
            fqh_v[g, :, at] = high
            fqm_v[g, :, at] = mid
            return 0

        lax.fori_loop(lo, hi, body, 0)

    gradient(0, 5)

    pltpu.make_async_copy(rs_buf, rs_buf, rs_r).wait()
    own = pl.ds(pl.multiple_of(y * 8, 8), 8)
    part = sum_v[SIDE - 1, own, :]
    for o in range(SIDE * SIDE - 1):
        part = part + rs_buf[o]
    zbuf[z] = part
    for dz in (1, 2, 3):
        pltpu.make_async_remote_copy(
            src_ref=zbuf.at[z], dst_ref=zbuf.at[z], send_sem=zs, recv_sem=zr,
            device_id=along_z(dz), device_id_type=MESH,
        ).start()

    gradient(5, 8)

    three = zbuf.at[pl.ds(0, 3)]
    pltpu.make_async_copy(three, three, zr).wait()
    at = pl.ds(pl.multiple_of(c * RANK + y * 8, 8), 8)
    lt_v[x, at, :] = (zbuf[0] + zbuf[1]) + (zbuf[2] + zbuf[3])
    for dx in range(SIDE):
        for dy in range(SIDE):
            if dx or dy:
                pltpu.make_async_remote_copy(
                    src_ref=lt_v.at[x, at, :], dst_ref=lt_v.at[x, at, :], send_sem=ag_s, recv_sem=ag_r.at[x],
                    device_id=plane(dx, dy), device_id_type=MESH,
                ).start()

    outs = []
    for g in range(SIDE):
        at = pl.ds(g * QUART, QUART)
        outs.append(pltpu.make_async_copy(fqh_v.at[g], fqh_o.at[:, at], out_s.at[0, g]))
        outs.append(pltpu.make_async_copy(fqm_v.at[g], fqm_o.at[:, at], out_s.at[1, g]))
        outs.append(pltpu.make_async_copy(fkv_v.at[g], fkv_o.at[at, :], out_s.at[2, g]))
    for cp in outs:
        cp.start()

    mine = pl.ds(pl.multiple_of(c * RANK, RANK), RANK)

    def forward(i):
        g = lax.rem(x + AG_ORDER[i], SIDE)
        return pltpu.make_async_remote_copy(
            src_ref=lt_v.at[g, mine, :], dst_ref=lt_v.at[g, mine, :], send_sem=fw_s.at[i], recv_sem=fw_r.at[i],
            device_id=partner, device_id_type=MESH,
        )

    accs = [jnp.zeros((CQ, 2 * RANK), F32), jnp.zeros((CQ, RANK), F32), jnp.zeros((2 * RANK, 2 * CKV), F32)]

    def term(i, accs):
        forward(i).wait()
        g = lax.rem(x + AG_ORDER[i], SIDE)
        high, mid = halves(lt_v[g])
        lst_v[g, :RANK, :] = high[:RANK]
        lst_v[g, RANK : 2 * RANK, :] = mid[:RANK]
        lst_v[g, 2 * RANK : 3 * RANK, :] = high[RANK:]
        lst_v[g, 3 * RANK :, :] = mid[RANK:]
        return [
            accs[0] + mm_t(fqh_v[g], lst_v[g, : 2 * RANK, :]),
            accs[1] + mm_t(fqm_v[g], lst_v[g, :RANK, :]),
            accs[2] + mm(lst_v[g, 2 * RANK :, :], fkv_v[g]),
        ]

    for i, dx in enumerate(AG_ORDER):
        g = lax.rem(x + dx, SIDE)
        got = rs_buf.at[pl.ds(0, SIDE if dx else SIDE - 1)]
        pltpu.make_async_copy(got, got, ag_r.at[g]).wait()
        forward(i).start()
        if i >= 1:
            accs = term(i - 1, accs)
    accs = term(SIDE - 1, accs)

    by_high = jnp.transpose(accs[0])
    yloc_v[:, CKV:COLS] = by_high[:RANK] + (by_high[RANK:] + jnp.transpose(accs[1]))
    yloc_v[:, :CKV] = accs[2][:RANK, :CKV] + (accs[2][RANK:, :CKV] + accs[2][:RANK, CKV:])
    yloc_v[:, COLS:] = jnp.zeros((RANK, WIDE - COLS), F32)

    my_rows = pl.ds(pl.multiple_of(c * 16, 16), 16)
    their_rows = pl.ds(pl.multiple_of((1 - c) * 16, 16), 16)
    cp = pltpu.make_async_remote_copy(
        src_ref=yloc_v.at[their_rows, :], dst_ref=yx_v, send_sem=y_s.at[0], recv_sem=y_r.at[0],
        device_id=partner, device_id_type=MESH,
    )
    cp.start()
    cp.wait()
    yz_v[z] = yloc_v[my_rows, :] + yx_v[...]
    for dz in (1, 2, 3):
        pltpu.make_async_remote_copy(
            src_ref=yz_v.at[z], dst_ref=yz_v.at[z], send_sem=y_s.at[1], recv_sem=y_r.at[1],
            device_id=along_z(dz), device_id_type=MESH,
        ).start()

    gram = jnp.zeros((2 * RANK, 2 * RANK), F32)
    for g in range(SIDE):
        full = lt_v[g]
        gram = gram + mm_t(full, full, precision=HIGHEST)
    gram_v[:, : 2 * RANK] = gram
    row = lax.broadcasted_iota(jnp.int32, (2 * RANK, 128), 0)
    lane = lax.broadcasted_iota(jnp.int32, (2 * RANK, 128), 1)
    gram_v[:, 2 * RANK :] = jnp.zeros((2 * RANK, 2 * RANK), F32)
    same = (row < RANK) == (lane < RANK)
    aug = jnp.where(lane < 2 * RANK, jnp.where(same, gram_v[...], 0.0), jnp.where(lane == row + 2 * RANK, 1.0, 0.0))
    inv_q = eliminate(aug[:RANK], 0)
    inv_kv = eliminate(aug[RANK:], RANK)
    gram_v[:RANK, :] = inv_q
    gram_v[RANK:, :] = inv_kv
    inv = gram_v[:, 2 * RANK :]
    left_copies = []
    for g in range(SIDE):
        lq_v[g, : 2 * RANK, :] = lst_v[g, : 2 * RANK, :]
        lq_v[g, 2 * RANK :, :] = lst_v[g, : 2 * RANK, :]
        kv = lst_v[g, 2 * RANK :, :]
        tkv_v[g] = jnp.transpose(jnp.concatenate([kv, kv], axis=0))
        at = pl.ds(g * QUART, QUART)
        left_copies.append(pltpu.make_async_copy(lq_v.at[g], lq_o.at[:, at], out_s.at[3, g]))
        left_copies.append(pltpu.make_async_copy(tkv_v.at[g], tkv_o.at[at, :], out_s.at[4, g]))
    for cp in left_copies:
        cp.start()

    three = yz_v.at[pl.ds(0, 3)]
    pltpu.make_async_copy(three, three, y_r.at[1]).wait()
    ysum_v[my_rows, :] = (yz_v[0] + yz_v[1]) + (yz_v[2] + yz_v[3])
    cp = pltpu.make_async_remote_copy(
        src_ref=ysum_v.at[my_rows, :], dst_ref=ysum_v.at[my_rows, :], send_sem=y_s.at[2], recv_sem=y_r.at[2],
        device_id=partner, device_id_type=MESH,
    )
    cp.start()
    cp.wait()

    total = ysum_v[...]
    is_kv = lax.broadcasted_iota(jnp.int32, (RANK, WIDE), 1) < CKV
    both = jnp.concatenate([jnp.where(is_kv, 0.0, total), jnp.where(is_kv, total, 0.0)], axis=0)
    new_t = jnp.dot(inv, both, precision=HIGHEST, preferred_element_type=F32) * (1.0 / 8.0)
    factor = tmm(inv, new_t, precision=HIGHEST)
    bn_v[...] = new_t[:RANK] + new_t[RANK:]
    high, mid = halves(factor)
    stack = jnp.concatenate([high[:RANK], high[:RANK], mid[:RANK], mid[:RANK]], axis=0)
    zq_v[...] = jnp.transpose(stack[:, CKV:COLS])
    zkv_v[...] = jnp.concatenate([high[RANK:], high[RANK:], mid[RANK:], mid[RANK:]], axis=0)[:, :CKV]
    last = [
        pltpu.make_async_copy(zq_v, zq_o, ld.at[0]),
        pltpu.make_async_copy(zkv_v, zkv_o, ld.at[1]),
        pltpu.make_async_copy(bn_v, bn_o, ld.at[2]),
    ]
    for cp in last:
        cp.start()

    pltpu.make_async_copy(rs_buf, rs_buf, rs_s).wait()
    three = zbuf.at[pl.ds(0, 3)]
    pltpu.make_async_copy(three, three, zs).wait()
    pltpu.make_async_copy(rs_buf, rs_buf, ag_s).wait()
    three = yz_v.at[pl.ds(0, 3)]
    pltpu.make_async_copy(three, three, y_s.at[1]).wait()
    for cp in outs + left_copies + last:
        cp.wait()


def reduce_call(act, ogq, ogkv, eq, ekv, bq, bkv):
    any_spec = pl.BlockSpec(memory_space=pl.ANY)
    hbm_spec = pl.BlockSpec(memory_space=pltpu.HBM)
    dma = pltpu.SemaphoreType.DMA
    v = pltpu.VMEM
    return pl.pallas_call(
        reduce_kernel,
        out_shape=[
            jax.ShapeDtypeStruct((CQ, D), BF16),
            jax.ShapeDtypeStruct((CQ, D), BF16),
            jax.ShapeDtypeStruct((D, 2 * CKV), BF16),
            jax.ShapeDtypeStruct((4 * RANK, D), BF16),
            jax.ShapeDtypeStruct((D, 4 * RANK), BF16),
            jax.ShapeDtypeStruct((CQ, 4 * RANK), BF16),
            jax.ShapeDtypeStruct((4 * RANK, CKV), BF16),
            jax.ShapeDtypeStruct((RANK, WIDE), F32),
        ],
        in_specs=[hbm_spec] * 7,
        out_specs=[any_spec] * 8,
        scratch_shapes=[
            v((SIDE, TOK, QUART), BF16),
            v((TOK, CKV), BF16),
            v((COLS, TOK), BF16),
            v((SIDE, CQ, QUART), BF16),
            v((SIDE, QUART, CKV), BF16),
            v((RANK, CQ), F32),
            v((RANK, CKV), F32),
            v((4 * RANK, TOK), BF16),
            v((2 * RANK, CQ), BF16),
            v((2 * RANK, CKV), BF16),
            v((SIDE, 2 * RANK, QUART), F32),
            v((SIDE, RANK, QUART), F32),
            v((SIDE, RANK, QUART), F32),
            v((SIDE * SIDE - 1, 8, QUART), F32),
            v((SIDE, 8, QUART), F32),
            v((SIDE, 2 * RANK, QUART), F32),
            v((SIDE, 4 * RANK, QUART), BF16),
            v((SIDE, 4 * RANK, QUART), BF16),
            v((SIDE, QUART, 4 * RANK), BF16),
            v((SIDE, CQ, QUART), BF16),
            v((SIDE, CQ, QUART), BF16),
            v((SIDE, QUART, 2 * CKV), BF16),
            v((RANK, WIDE), F32),
            v((16, WIDE), F32),
            v((SIDE, 16, WIDE), F32),
            v((RANK, WIDE), F32),
            v((2 * RANK, 128), F32),
            v((CQ, 4 * RANK), BF16),
            v((4 * RANK, CKV), BF16),
            v((RANK, WIDE), F32),
            dma((4,)), dma((SIDE, 3)),
            dma((SIDE,)), dma((SIDE,)),
            dma, dma, dma, dma,
            dma, dma((SIDE,)), dma((SIDE,)), dma((SIDE,)),
            dma((3,)), dma((3,)), dma((5, SIDE)),
        ],
        compiler_params=pltpu.CompilerParams(collective_id=0, has_side_effects=True, vmem_limit_bytes=40 * MIB),
        name="left_and_right_factors",
    )(act, ogq, ogkv, eq, ekv, bq, bkv)


def write_kernel(fqh, fqm, fkv, lq, tkv, zq, zkv, bn, uq, ukv, eq, ekv, bq, bkv):
    approx = mm(zq[...], lq[...])
    uq[...] = approx.astype(BF16)
    eq[0] = (fqh[...].astype(F32) + fqm[...].astype(F32) - approx).astype(BF16)
    approx = mm(tkv[...], zkv[...])
    ukv[...] = approx.astype(BF16)
    ekv[0] = (fkv[:, :CKV].astype(F32) + fkv[:, CKV:].astype(F32) - approx).astype(BF16)

    @pl.when(pl.program_id(0) == 0)
    def _():
        bkv[...] = bn[:, :CKV]
        bq[...] = bn[:, CKV:COLS]


def write_call(fqh, fqm, fkv, lq, tkv, zq, zkv, bn, step=640):
    by_row = lambda cols: pl.BlockSpec((step, cols), lambda i: (i, 0))
    by_lane = lambda rows: pl.BlockSpec((rows, step), lambda i: (0, i))
    whole = lambda *shape: pl.BlockSpec(shape, lambda i: (0,) * len(shape))
    return pl.pallas_call(
        write_kernel,
        grid=(D // step,),
        out_shape=[
            jax.ShapeDtypeStruct((CQ, D), BF16),
            jax.ShapeDtypeStruct((D, CKV), BF16),
            jax.ShapeDtypeStruct((1, CQ, D), BF16),
            jax.ShapeDtypeStruct((1, D, CKV), BF16),
            jax.ShapeDtypeStruct((RANK, CQ), F32),
            jax.ShapeDtypeStruct((RANK, CKV), F32),
        ],
        in_specs=[
            by_lane(CQ), by_lane(CQ), by_row(2 * CKV), by_lane(4 * RANK), by_row(4 * RANK),
            whole(CQ, 4 * RANK), whole(4 * RANK, CKV), whole(RANK, WIDE),
        ],
        out_specs=[
            by_lane(CQ),
            by_row(CKV),
            pl.BlockSpec((1, CQ, step), lambda i: (0, 0, i)),
            pl.BlockSpec((1, step, CKV), lambda i: (0, i, 0)),
            whole(RANK, CQ),
            whole(RANK, CKV),
        ],
        compiler_params=pltpu.CompilerParams(vmem_limit_bytes=24 * MIB),
        name="updates_and_errors",
    )(fqh, fqm, fkv, lq, tkv, zq, zkv, bn)


def local(act, ogq, ogkv, eq, ekv, bq, bkv):
    turned = lambda a: jnp.swapaxes(a, -1, -2)
    got = reduce_call(act, turned(ogq), ogkv, turned(eq), ekv, turned(bq), turned(bkv))
    uq, ukv, eq, ekv, bq, bkv = write_call(*got)
    return (turned(uq), ukv, turned(eq), ekv, turned(bq), turned(bkv))


def solution(mesh):
    placed = (
        P("dp", None, None),
        P("dp", None, "tensor"),
        P("dp", None, "tensor"),
        P("dp", None, "tensor"),
        P("dp", None, "tensor"),
        P("tensor", None),
        P("tensor", None),
    )
    return jax.shard_map(
        local,
        mesh=mesh,
        in_specs=placed,
        out_specs=(
            P(None, "tensor"),
            P(None, "tensor"),
            P("dp", None, "tensor"),
            P("dp", None, "tensor"),
            P("tensor", None),
            P("tensor", None),
        ),
        check_vma=False,
    )
```

```python
import functools

import jax
import jax.numpy as jnp
from jax import lax
from jax.experimental import pallas as pl
from jax.experimental.pallas import tpu as pltpu
from jax.sharding import PartitionSpec as P

F32 = jnp.float32
BF16 = jnp.bfloat16
MESH = pl.DeviceIdType.MESH
HIGHEST = lax.Precision.HIGHEST
MIB = 1 << 20

SIDE = 4
D = 5120
WIDTHS = (768, 512)
STARTS = (0, SIDE * 768)
TOK = 1024
CQ, CKV = 320, 128
COLS = CQ + CKV
RANK = 32
WIDE = 512
ROT = (1, 3, 2, 0)
AG_ORDER = (0, 1, 3, 2)
UNITS = [(h, k) for h in range(2) for k in range(SIDE)]


def mm(a, b):
    return jnp.dot(a, b, preferred_element_type=F32)


def mm_t(a, b, precision=None):
    return lax.dot_general(a, b, (((1,), (1,)), ((), ())), preferred_element_type=F32, precision=precision)


def tmm(a, b, precision=None):
    return lax.dot_general(a, b, (((0,), (0,)), ((), ())), preferred_element_type=F32, precision=precision)


def halves(v):
    high = v.astype(BF16)
    return high, (v - high.astype(F32)).astype(BF16)


def eliminate(a, off):
    row = lax.broadcasted_iota(jnp.int32, (RANK, 128), 0)
    lane = lax.broadcasted_iota(jnp.int32, (RANK, 128), 1)
    for k in range(RANK - 1):
        col = jnp.broadcast_to(a[:, off + k : off + k + 1], (RANK, 128))
        scaled = a[k : k + 1, :] / col[k : k + 1, :]
        a = a - jnp.where(row > k, col, 0.0) * scaled
    diag = jnp.sum(jnp.where(lane == row + off, a, 0.0), axis=1, keepdims=True)
    return a * lax.rsqrt(diag)


def reduce_kernel(
    act, ogq, ogkv, eq, ekv, bq, bkv,
    fqh0, fqh1, fqm0, fqm1, fkv0, fkv1, lq0, lq1, tkv0, tkv1, zq_o, zkv_o, bn_o,
    act0, act1, eq0, eq1, ekv0, ekv1, loc0, loc1, xr0, xr1, sum0, sum1, rs0, rs1, zb0, zb1, lt0, lt1,
    ogkv_v, og_v, bq_v, bkv_v, pst_v, bq2_v, bkv2_v, yloc_v, yx_v, yz_v, ysum_v, gram_v,
    ld, lda, xs, xr, rs_s, rs_r, zs, zr, ag_s, ag_r, fw_s, fw_r, y_s, y_r,
):
    fqh, fqm, fkv, lq, tkv = (fqh0, fqh1), (fqm0, fqm1), (fkv0, fkv1), (lq0, lq1), (tkv0, tkv1)
    act_v, eq_v, ekv_v, loc_v, xr_v = (act0, act1), (eq0, eq1), (ekv0, ekv1), (loc0, loc1), (xr0, xr1)
    sum_v, rs_buf, zbuf, lt_v = (sum0, sum1), (rs0, rs1), (zb0, zb1), (lt0, lt1)

    dp, t = lax.axis_index("dp"), lax.axis_index("tensor")
    z, c = dp // 2, lax.rem(dp, 2)
    x, y = t // SIDE, lax.rem(t, SIDE)
    partner = (z * 2 + 1 - c, t)

    def plane(dx, dy):
        return (dp, lax.rem(x + dx, SIDE) * SIDE + lax.rem(y + dy, SIDE))

    def along_z(dz):
        return (lax.rem(z + dz, SIDE) * 2 + c, t)

    def part_of(rows, size):
        return pl.ds(pl.multiple_of(rows * size, size), size)

    def remote(src, dst, send, recv, device):
        return pltpu.make_async_remote_copy(
            src_ref=src, dst_ref=dst, send_sem=send, recv_sem=recv, device_id=device, device_id_type=MESH
        )

    def wait_for(ref, sem):
        pltpu.make_async_copy(ref, ref, sem).wait()

    def load(u):
        h, k = UNITS[u]
        g = lax.rem(x + ROT[k], SIDE)
        at = pl.ds(pl.multiple_of(STARTS[h] + g * WIDTHS[h], 256), WIDTHS[h])
        return [
            pltpu.make_async_copy(act.at[0, :, at], act_v[h].at[g], lda.at[u, 0]),
            pltpu.make_async_copy(eq.at[0, :, at], eq_v[h].at[g], lda.at[u, 1]),
            pltpu.make_async_copy(ekv.at[0, at, :], ekv_v[h].at[g], lda.at[u, 2]),
        ]

    first = [
        pltpu.make_async_copy(src, dst, ld.at[i])
        for i, (src, dst) in enumerate(
            [(ogq.at[0], og_v.at[pl.ds(CKV, CQ), :]), (ogkv.at[0], ogkv_v), (bq, bq_v), (bkv, bkv_v)]
        )
    ]
    for cp in first + load(0) + load(1):
        cp.start()

    barrier = pltpu.get_barrier_semaphore()
    peers = [partner]
    peers += [plane(dx, dy) for dx in range(SIDE) for dy in range(SIDE) if dx or dy]
    peers += [along_z(dz) for dz in (1, 2, 3)]
    for p in peers:
        pl.semaphore_signal(barrier, inc=1, device_id=p, device_id_type=MESH)

    for cp in first:
        cp.wait()
    og_v[:CKV, :] = jnp.transpose(ogkv_v[...])
    for src, b2, og_rows, base in ((bq_v, bq2_v, slice(CKV, COLS), 0), (bkv_v, bkv2_v, slice(0, CKV), 2 * RANK)):
        bt = src[...]
        high, mid = halves(bt)
        low = (bt - high.astype(F32) - mid.astype(F32)).astype(BF16)
        b2[:RANK, :] = high
        b2[RANK:, :] = mid
        og_w = og_v[og_rows, :]
        proj = mm(high, og_w) + (mm(mid, og_w) + mm(low, og_w))
        p_high, p_mid = halves(proj)
        pst_v[base : base + RANK, :] = p_high
        pst_v[base + RANK : base + 2 * RANK, :] = p_mid

    my_half, their_half = part_of(c, RANK), part_of(1 - c, RANK)

    def exchange(u):
        h, k = UNITS[u]
        return remote(loc_v[h].at[k, their_half, :], xr_v[h].at[k], xs.at[u], xr.at[u], partner)

    def scatter(u):
        h, k = UNITS[u]
        exchange(u).wait()
        sum_v[h][k] = loc_v[h][k, my_half, :] + xr_v[h][k]
        for dy in range(SIDE):
            if ROT[k] or dy:
                rows = part_of(lax.rem(y + dy, SIDE), 8)
                remote(
                    sum_v[h].at[k, rows, :], rs_buf[h].at[ROT[k] * SIDE + dy - 1], rs_s.at[h], rs_r.at[h],
                    plane(ROT[k], dy),
                ).start()

    for u, (h, k) in enumerate(UNITS):
        g = lax.rem(x + ROT[k], SIDE)
        for cp in load(u):
            cp.wait()
        if u + 2 < len(UNITS):
            for cp in load(u + 2):
                cp.start()
        bq2, bkv2 = bq2_v[...], bkv2_v[...]
        pst = pst_v[...]
        for i in range(WIDTHS[h] // 256):
            cut = slice(i * 256, (i + 1) * 256)
            prod = mm(pst, act_v[h][g, :, cut])
            from_q = mm(bq2, eq_v[h][g, :, cut])
            from_kv = mm_t(bkv2, ekv_v[h][g, cut, :])
            loc_v[h][k, :RANK, cut] = (prod[:RANK] + prod[RANK : 2 * RANK]) + (from_q[:RANK] + from_q[RANK:])
            loc_v[h][k, RANK:, cut] = (prod[2 * RANK : 3 * RANK] + prod[3 * RANK :]) + (from_kv[:RANK] + from_kv[RANK:])
        if u == 0:
            pl.semaphore_wait(barrier, len(peers))
        exchange(u).start()
        if u >= 1:
            scatter(u - 1)
    scatter(len(UNITS) - 1)

    def gradient(h, lo, hi):
        blocks = WIDTHS[h] // 256

        def body(i, _):
            g = i // blocks
            at = pl.ds(pl.multiple_of(lax.rem(i, blocks) * 256, 256), 256)
            grads = mm(og_v[...], act_v[h][g, :, at])
            high, mid = halves(jnp.transpose(grads[:CKV]) + ekv_v[h][g, at, :].astype(F32))
            fkv[h][g, at, :CKV] = high
            fkv[h][g, at, CKV:] = mid
            high, mid = halves(grads[CKV:] + eq_v[h][g, :, at].astype(F32))
            fqh[h][g, :, at] = high
            fqm[h][g, :, at] = mid
            return 0

        lax.fori_loop(lo * blocks, hi * blocks, body, 0)

    def sum_plane(h):
        wait_for(rs_buf[h], rs_r.at[h])
        part = sum_v[h][SIDE - 1, part_of(y, 8), :]
        for o in range(SIDE * SIDE - 1):
            part = part + rs_buf[h][o]
        zbuf[h][z] = part
        for dz in (1, 2, 3):
            remote(zbuf[h].at[z], zbuf[h].at[z], zs.at[h], zr.at[h], along_z(dz)).start()

    own = part_of(c * SIDE + y, 8)

    def gather(h):
        wait_for(zbuf[h].at[pl.ds(0, 3)], zr.at[h])
        lt_v[h][x, own, :] = (zbuf[h][0] + zbuf[h][1]) + (zbuf[h][2] + zbuf[h][3])
        for dx in AG_ORDER:
            for dy in range(SIDE):
                if dx or dy:
                    piece = lt_v[h].at[x, own, :]
                    remote(piece, piece, ag_s.at[h], ag_r.at[h * SIDE + x], plane(dx, dy)).start()

    gradient(0, 0, 1)
    sum_plane(0)
    gradient(0, 1, 3)
    sum_plane(1)
    gather(0)
    gradient(0, 3, 4)
    gradient(1, 0, 2)
    gather(1)
    gradient(1, 2, 4)

    def chunk_of(u):
        return lax.rem(x + AG_ORDER[u % SIDE], SIDE)

    def forward(u):
        piece = lt_v[u // SIDE].at[chunk_of(u), my_half, :]
        return remote(piece, piece, fw_s.at[u], fw_r.at[u], partner)

    def term(u, accs):
        h, g = u // SIDE, chunk_of(u)
        forward(u).wait()
        left = lt_v[h][g]
        high, mid = halves(left)
        q = jnp.concatenate([high[:RANK], mid[:RANK]], axis=0)
        kv = jnp.concatenate([high[RANK:], mid[RANK:]], axis=0)
        lq[h][g, : 2 * RANK, :] = q
        lq[h][g, 2 * RANK :, :] = q
        tkv[h][g] = jnp.transpose(jnp.concatenate([kv, kv], axis=0))
        return [
            accs[0] + mm_t(fqh[h][g], q),
            accs[1] + mm_t(fqm[h][g], high[:RANK]),
            accs[2] + mm(kv, fkv[h][g]),
            accs[3] + mm_t(left, left, precision=HIGHEST),
        ]

    accs = [
        jnp.zeros((CQ, 2 * RANK), F32),
        jnp.zeros((CQ, RANK), F32),
        jnp.zeros((2 * RANK, 2 * CKV), F32),
        jnp.zeros((2 * RANK, 2 * RANK), F32),
    ]
    for u in range(2 * SIDE):
        h = u // SIDE
        got = rs_buf[h].at[pl.ds(0, SIDE if AG_ORDER[u % SIDE] else SIDE - 1)]
        wait_for(got, ag_r.at[h * SIDE + chunk_of(u)])
        forward(u).start()
        if u >= 1:
            accs = term(u - 1, accs)
    accs = term(2 * SIDE - 1, accs)

    by_high = jnp.transpose(accs[0])
    yloc_v[:, CKV:COLS] = by_high[:RANK] + (by_high[RANK:] + jnp.transpose(accs[1]))
    yloc_v[:, :CKV] = accs[2][:RANK, :CKV] + (accs[2][RANK:, :CKV] + accs[2][:RANK, CKV:])
    yloc_v[:, COLS:] = jnp.zeros((RANK, WIDE - COLS), F32)

    my_rows, their_rows = part_of(c, 16), part_of(1 - c, 16)
    cp = remote(yloc_v.at[their_rows, :], yx_v, y_s.at[0], y_r.at[0], partner)
    cp.start()
    cp.wait()
    yz_v[z] = yloc_v[my_rows, :] + yx_v[...]
    for dz in (1, 2, 3):
        remote(yz_v.at[z], yz_v.at[z], y_s.at[1], y_r.at[1], along_z(dz)).start()

    gram_v[:, : 2 * RANK] = accs[3]
    gram_v[:, 2 * RANK :] = jnp.zeros((2 * RANK, 2 * RANK), F32)
    row = lax.broadcasted_iota(jnp.int32, (2 * RANK, 128), 0)
    lane = lax.broadcasted_iota(jnp.int32, (2 * RANK, 128), 1)
    same = (row < RANK) == (lane < RANK)
    aug = jnp.where(lane < 2 * RANK, jnp.where(same, gram_v[...], 0.0), jnp.where(lane == row + 2 * RANK, 1.0, 0.0))
    gram_v[:RANK, :] = eliminate(aug[:RANK], 0)
    gram_v[RANK:, :] = eliminate(aug[RANK:], RANK)
    inv = gram_v[:, 2 * RANK :]

    three = yz_v.at[pl.ds(0, 3)]
    wait_for(three, y_r.at[1])
    ysum_v[my_rows, :] = (yz_v[0] + yz_v[1]) + (yz_v[2] + yz_v[3])
    cp = remote(ysum_v.at[my_rows, :], ysum_v.at[my_rows, :], y_s.at[2], y_r.at[2], partner)
    cp.start()
    cp.wait()

    total = ysum_v[...]
    is_kv = lax.broadcasted_iota(jnp.int32, (RANK, WIDE), 1) < CKV
    both = jnp.concatenate([jnp.where(is_kv, 0.0, total), jnp.where(is_kv, total, 0.0)], axis=0)
    new_t = jnp.dot(inv, both, precision=HIGHEST, preferred_element_type=F32) * (1.0 / 8.0)
    factor = tmm(inv, new_t, precision=HIGHEST)
    bn_o[...] = new_t[:RANK] + new_t[RANK:]
    high, mid = halves(factor)
    stack = jnp.concatenate([high[:RANK], high[:RANK], mid[:RANK], mid[:RANK]], axis=0)
    zq_o[...] = jnp.transpose(stack[:, CKV:COLS])
    zkv_o[...] = jnp.concatenate([high[RANK:], high[RANK:], mid[RANK:], mid[RANK:]], axis=0)[:, :CKV]

    for h in range(2):
        wait_for(rs_buf[h], rs_s.at[h])
        wait_for(zbuf[h].at[pl.ds(0, 3)], zs.at[h])
        wait_for(rs_buf[h], ag_s.at[h])
    wait_for(three, y_s.at[1])


def reduce_call(*args):
    any_spec = pl.BlockSpec(memory_space=pl.ANY)
    vmem_spec = pl.BlockSpec(memory_space=pltpu.VMEM)
    dma = pltpu.SemaphoreType.DMA
    v = pltpu.VMEM
    pair = lambda shape, dtype: [v(tuple(w if n is None else n for n in shape), dtype) for w in WIDTHS]
    outs = [
        *pair((SIDE, CQ, None), BF16),
        *pair((SIDE, CQ, None), BF16),
        *pair((SIDE, None, 2 * CKV), BF16),
        *pair((SIDE, 4 * RANK, None), BF16),
        *pair((SIDE, None, 4 * RANK), BF16),
        v((CQ, 4 * RANK), BF16),
        v((4 * RANK, CKV), BF16),
        v((RANK, WIDE), F32),
    ]
    return pl.pallas_call(
        reduce_kernel,
        out_shape=[jax.ShapeDtypeStruct(o.shape, o.dtype) for o in outs],
        in_specs=[any_spec] * 7,
        out_specs=[vmem_spec] * len(outs),
        scratch_shapes=[
            *pair((SIDE, TOK, None), BF16),
            *pair((SIDE, CQ, None), BF16),
            *pair((SIDE, None, CKV), BF16),
            *pair((SIDE, 2 * RANK, None), F32),
            *pair((SIDE, RANK, None), F32),
            *pair((SIDE, RANK, None), F32),
            *pair((SIDE * SIDE - 1, 8, None), F32),
            *pair((SIDE, 8, None), F32),
            *pair((SIDE, 2 * RANK, None), F32),
            v((TOK, CKV), BF16),
            v((COLS, TOK), BF16),
            v((RANK, CQ), F32),
            v((RANK, CKV), F32),
            v((4 * RANK, TOK), BF16),
            v((2 * RANK, CQ), BF16),
            v((2 * RANK, CKV), BF16),
            v((RANK, WIDE), F32),
            v((16, WIDE), F32),
            v((SIDE, 16, WIDE), F32),
            v((RANK, WIDE), F32),
            v((2 * RANK, 128), F32),
            dma((4,)), dma((2 * SIDE, 3)),
            dma((2 * SIDE,)), dma((2 * SIDE,)),
            dma((2,)), dma((2,)), dma((2,)), dma((2,)),
            dma((2,)), dma((2 * SIDE,)), dma((2 * SIDE,)), dma((2 * SIDE,)),
            dma((3,)), dma((3,)),
        ],
        compiler_params=pltpu.CompilerParams(collective_id=0, has_side_effects=True, vmem_limit_bytes=40 * MIB),
        name="left_and_right_factors",
    )(*[pltpu.with_memory_space_constraint(a, pltpu.HBM) for a in args])


def write_kernel(
    fqh0, fqh1, fqm0, fqm1, fkv0, fkv1, lq0, lq1, tkv0, tkv1, zq, zkv, bn,
    uq, ukv, eq, ekv, bq, bkv,
    uq0, uq1, ukv0, ukv1, eq0, eq1, ekv0, ekv1, sem,
):
    halved = (
        (fqh0, fqm0, fkv0, lq0, tkv0, uq0, ukv0, eq0, ekv0),
        (fqh1, fqm1, fkv1, lq1, tkv1, uq1, ukv1, eq1, ekv1),
    )
    copies = []
    for h, (fqh, fqm, fkv, lq, tkv, uq_v, ukv_v, eq_v, ekv_v) in enumerate(halved):
        for g in range(SIDE):
            approx = mm(zq[...], lq[g])
            uq_v[g] = approx.astype(BF16)
            eq_v[g] = (fqh[g].astype(F32) + fqm[g].astype(F32) - approx).astype(BF16)
            approx = mm(tkv[g], zkv[...])
            ukv_v[g] = approx.astype(BF16)
            ekv_v[g] = (fkv[g, :, :CKV].astype(F32) + fkv[g, :, CKV:].astype(F32) - approx).astype(BF16)
            at = pl.ds(STARTS[h] + g * WIDTHS[h], WIDTHS[h])
            pairs = [(uq_v, uq.at[:, at]), (ukv_v, ukv.at[at, :]), (eq_v, eq.at[0, :, at]), (ekv_v, ekv.at[0, at, :])]
            for i, (src, dst) in enumerate(pairs):
                cp = pltpu.make_async_copy(src.at[g], dst, sem.at[h * SIDE + g, i])
                cp.start()
                copies.append(cp)
    bkv[...] = bn[:, :CKV]
    bq[...] = bn[:, CKV:COLS]
    for cp in copies:
        cp.wait()


def write_call(*args):
    vmem_spec = pl.BlockSpec(memory_space=pltpu.VMEM)
    any_spec = pl.BlockSpec(memory_space=pl.ANY)
    pair = lambda *shape: [pltpu.VMEM(tuple(w if n is None else n for n in shape), BF16) for w in WIDTHS]
    return pl.pallas_call(
        write_kernel,
        out_shape=[
            jax.ShapeDtypeStruct((CQ, D), BF16),
            jax.ShapeDtypeStruct((D, CKV), BF16),
            jax.ShapeDtypeStruct((1, CQ, D), BF16),
            jax.ShapeDtypeStruct((1, D, CKV), BF16),
            jax.ShapeDtypeStruct((RANK, CQ), F32),
            jax.ShapeDtypeStruct((RANK, CKV), F32),
        ],
        in_specs=[vmem_spec] * len(args),
        out_specs=[any_spec] * 4 + [vmem_spec] * 2,
        scratch_shapes=[
            *pair(SIDE, CQ, None),
            *pair(SIDE, None, CKV),
            *pair(SIDE, CQ, None),
            *pair(SIDE, None, CKV),
            pltpu.SemaphoreType.DMA((2 * SIDE, 4)),
        ],
        compiler_params=pltpu.CompilerParams(vmem_limit_bytes=24 * MIB),
        name="updates_and_errors",
    )(*args)


def local(act, ogq, ogkv, eq, ekv, bq, bkv):
    turned = lambda a: jnp.swapaxes(a, -1, -2)
    got = reduce_call(act, turned(ogq), ogkv, turned(eq), ekv, turned(bq), turned(bkv))
    uq, ukv, eq, ekv, bq, bkv = write_call(*got)
    return (turned(uq), ukv, turned(eq), ekv, turned(bq), turned(bkv))


def solution(mesh):
    placed = (
        P("dp", None, None),
        P("dp", None, "tensor"),
        P("dp", None, "tensor"),
        P("dp", None, "tensor"),
        P("dp", None, "tensor"),
        P("tensor", None),
        P("tensor", None),
    )
    return jax.shard_map(
        local,
        mesh=mesh,
        in_specs=placed,
        out_specs=(
            P(None, "tensor"),
            P(None, "tensor"),
            P("dp", None, "tensor"),
            P("dp", None, "tensor"),
            P("tensor", None),
            P("tensor", None),
        ),
        check_vma=False,
    )
```

```python
import functools

import jax
import jax.numpy as jnp
from jax import lax
from jax.experimental import pallas as pl
from jax.experimental.pallas import tpu as pltpu
from jax.sharding import PartitionSpec as P

F32 = jnp.float32
BF16 = jnp.bfloat16
MESH = pl.DeviceIdType.MESH
HIGHEST = lax.Precision.HIGHEST
MIB = 1 << 20

SIDE = 4
D = 5120
WIDTHS = (512, 384, 384)
PARTS = len(WIDTHS)
STARTS = tuple(SIDE * sum(WIDTHS[:h]) for h in range(PARTS))
TOK = 1024
CQ, CKV = 320, 128
COLS = CQ + CKV
RANK = 32
WIDE = 512
ROT = (1, 3, 2, 0)
AG_ORDER = (0, 1, 3, 2)
AHEAD = 3
GATE = 4
LAG = 2
UNITS = [(h, k) for h in range(PARTS) for k in range(SIDE)]


def mm(a, b):
    return jnp.dot(a, b, preferred_element_type=F32)


def mm_t(a, b, precision=None):
    return lax.dot_general(a, b, (((1,), (1,)), ((), ())), preferred_element_type=F32, precision=precision)


def tmm(a, b, precision=None):
    return lax.dot_general(a, b, (((0,), (0,)), ((), ())), preferred_element_type=F32, precision=precision)


def halves(v):
    high = v.astype(BF16)
    return high, (v - high.astype(F32)).astype(BF16)


def eliminate(a, off):
    row = lax.broadcasted_iota(jnp.int32, (RANK, 128), 0)
    lane = lax.broadcasted_iota(jnp.int32, (RANK, 128), 1)
    for k in range(RANK - 1):
        col = jnp.broadcast_to(a[:, off + k : off + k + 1], (RANK, 128))
        scaled = a[k : k + 1, :] / col[k : k + 1, :]
        a = a - jnp.where(row > k, col, 0.0) * scaled
    diag = jnp.sum(jnp.where(lane == row + off, a, 0.0), axis=1, keepdims=True)
    return a * lax.rsqrt(diag)


def by_part(refs, count):
    return [refs[i * PARTS : (i + 1) * PARTS] for i in range(count)], refs[count * PARTS :]


def reduce_kernel(act, ogq, ogkv, eq, ekv, bq, bkv, *refs):
    (fqh, fqm, fkv, lq, tkv), refs = by_part(refs, 5)
    zq_o, zkv_o, bn_o, *refs = refs
    (act_v, eq_v, ekv_v, loc_v, xr_v, sum_v, rs_buf, zbuf, lt_v), refs = by_part(refs, 9)
    ogkv_v, og_v, bq_v, bkv_v, pst_v, bq2_v, bkv2_v, yloc_v, yx_v, yz_v, ysum_v, gram_v, *refs = refs
    ld, lda, xs, xr, rs_s, rs_r, zs, zr, ag_s, ag_r, fw_s, fw_r, y_s, y_r = refs

    dp, t = lax.axis_index("dp"), lax.axis_index("tensor")
    z, c = dp // 2, lax.rem(dp, 2)
    x, y = t // SIDE, lax.rem(t, SIDE)
    partner = (z * 2 + 1 - c, t)

    spots = ((x, y, z), (y, z, x), (z, x, y))

    def moved(d):
        return (lax.rem(z + d[2], SIDE) * 2 + c, lax.rem(x + d[0], SIDE) * SIDE + lax.rem(y + d[1], SIDE))

    def plane(h, d1, d2):
        return moved(((d1, d2, 0), (0, d1, d2), (d2, 0, d1))[h])

    def along(h, d):
        return moved(((0, 0, d), (d, 0, 0), (0, d, 0))[h])

    def part_of(rows, size):
        return pl.ds(pl.multiple_of(rows * size, size), size)

    def remote(src, dst, send, recv, device):
        return pltpu.make_async_remote_copy(
            src_ref=src, dst_ref=dst, send_sem=send, recv_sem=recv, device_id=device, device_id_type=MESH
        )

    def wait_for(ref, sem):
        pltpu.make_async_copy(ref, ref, sem).wait()

    def load(u):
        h, k = UNITS[u]
        g = lax.rem(spots[h][0] + ROT[k], SIDE)
        at = pl.ds(pl.multiple_of(STARTS[h] + g * WIDTHS[h], 128), WIDTHS[h])
        return pltpu.make_async_copy(act.at[0, :, at], act_v[h].at[g], lda.at[u])

    def load_errors(h):
        at = pl.ds(STARTS[h], SIDE * WIDTHS[h])
        return [
            pltpu.make_async_copy(eq.at[0, :, at], eq_v[h], ld.at[4 + 2 * h]),
            pltpu.make_async_copy(ekv.at[0, at, :], ekv_v[h], ld.at[5 + 2 * h]),
        ]

    first = [
        pltpu.make_async_copy(src, dst, ld.at[i])
        for i, (src, dst) in enumerate(
            [(ogq.at[0], og_v.at[pl.ds(CKV, CQ), :]), (ogkv.at[0], ogkv_v), (bq, bq_v), (bkv, bkv_v)]
        )
    ]
    for cp in first + load_errors(0) + [load(u) for u in range(AHEAD)]:
        cp.start()

    barrier = pltpu.get_barrier_semaphore()
    peers = [partner]
    peers += [moved((i, j, 0)) for i in range(SIDE) for j in range(SIDE) if i or j]
    peers += [moved((i, 0, j)) for i in range(SIDE) for j in (1, 2, 3)]
    peers += [moved((0, i, j)) for i in (1, 2, 3) for j in (1, 2, 3)]
    for p in peers:
        pl.semaphore_signal(barrier, inc=1, device_id=p, device_id_type=MESH)

    for cp in first:
        cp.wait()
    og_v[:CKV, :] = jnp.transpose(ogkv_v[...])
    for src, b2, og_rows, base in ((bq_v, bq2_v, slice(CKV, COLS), 0), (bkv_v, bkv2_v, slice(0, CKV), 2 * RANK)):
        bt = src[...]
        high, mid = halves(bt)
        low = (bt - high.astype(F32) - mid.astype(F32)).astype(BF16)
        b2[:RANK, :] = high
        b2[RANK:, :] = mid
        og_w = og_v[og_rows, :]
        proj = mm(high, og_w) + (mm(mid, og_w) + mm(low, og_w))
        p_high, p_mid = halves(proj)
        pst_v[base : base + RANK, :] = p_high
        pst_v[base + RANK : base + 2 * RANK, :] = p_mid

    my_half, their_half = part_of(c, RANK), part_of(1 - c, RANK)

    def exchange(u):
        h, k = UNITS[u]
        return remote(loc_v[h].at[k, their_half, :], xr_v[h].at[k], xs.at[u], xr.at[u], partner)

    def scatter(u):
        h, k = UNITS[u]
        exchange(u).wait()
        sum_v[h][k] = loc_v[h][k, my_half, :] + xr_v[h][k]
        for dy in range(SIDE):
            if ROT[k] or dy:
                rows = part_of(lax.rem(spots[h][1] + dy, SIDE), 8)
                remote(
                    sum_v[h].at[k, rows, :], rs_buf[h].at[ROT[k] * SIDE + dy - 1], rs_s.at[h], rs_r.at[h],
                    plane(h, ROT[k], dy),
                ).start()

    for u, (h, k) in enumerate(UNITS):
        g = lax.rem(spots[h][0] + ROT[k], SIDE)
        load(u).wait()
        if k == 0:
            for cp in load_errors(h):
                cp.wait()
        if k == 1 and h + 1 < PARTS:
            for cp in load_errors(h + 1):
                cp.start()
        for later in range(u + AHEAD, min(u + AHEAD + 1, len(UNITS)) if u < GATE else len(UNITS) if u == GATE else 0):
            load(later).start()
        bq2, bkv2 = bq2_v[...], bkv2_v[...]
        pst = pst_v[...]
        at = pl.ds(pl.multiple_of(g * WIDTHS[h], 128), WIDTHS[h])
        prod = mm(pst, act_v[h][g])
        from_q = mm(bq2, eq_v[h][:, at])
        from_kv = mm_t(bkv2, ekv_v[h][at, :])
        loc_v[h][k, :RANK, :] = (prod[:RANK] + prod[RANK : 2 * RANK]) + (from_q[:RANK] + from_q[RANK:])
        loc_v[h][k, RANK:, :] = (prod[2 * RANK : 3 * RANK] + prod[3 * RANK :]) + (from_kv[:RANK] + from_kv[RANK:])
        if u == GATE:
            pl.semaphore_wait(barrier, len(peers))
            for v in range(GATE):
                exchange(v).start()
        if u >= GATE:
            exchange(u).start()
        if u > GATE:
            for v in range(max(0, u - LAG) if u > GATE + 1 else 0, u - LAG + 1):
                scatter(v)
    for v in range(len(UNITS) - LAG, len(UNITS)):
        scatter(v)

    def gradient(h, lo, hi):
        width = WIDTHS[h]

        def body(g, _):
            at = pl.ds(pl.multiple_of(g * width, width), width)
            grads = mm(og_v[...], act_v[h][g])
            high, mid = halves(jnp.transpose(grads[:CKV]) + ekv_v[h][at, :].astype(F32))
            fkv[h][g, :, :CKV] = high
            fkv[h][g, :, CKV:] = mid
            high, mid = halves(grads[CKV:] + eq_v[h][:, at].astype(F32))
            fqh[h][g] = high
            fqm[h][g] = mid
            return 0

        lax.fori_loop(lo, hi, body, 0)

    def sum_plane(h):
        wait_for(rs_buf[h], rs_r.at[h])
        part = sum_v[h][SIDE - 1, part_of(spots[h][1], 8), :]
        for o in range(SIDE * SIDE - 1):
            part = part + rs_buf[h][o]
        here = spots[h][2]
        zbuf[h][here] = part
        for d in (1, 2, 3):
            remote(zbuf[h].at[here], zbuf[h].at[here], zs.at[h], zr.at[h], along(h, d)).start()

    def gather(h):
        wait_for(zbuf[h].at[pl.ds(0, 3)], zr.at[h])
        g, own = spots[h][0], part_of(c * SIDE + spots[h][1], 8)
        lt_v[h][g, own, :] = (zbuf[h][0] + zbuf[h][1]) + (zbuf[h][2] + zbuf[h][3])
        for d1 in AG_ORDER:
            for d2 in range(SIDE):
                if d1 or d2:
                    piece = lt_v[h].at[g, own, :]
                    remote(piece, piece, ag_s.at[h], ag_r.at[h * SIDE + g], plane(h, d1, d2)).start()

    gradient(0, 0, 2)
    sum_plane(0)
    gradient(0, 2, 3)
    sum_plane(1)
    gradient(0, 3, 4)
    gather(0)
    sum_plane(2)
    gradient(1, 0, 2)
    gather(1)
    gradient(1, 2, 4)
    gather(2)
    gradient(2, 0, 2)

    def chunk_of(u):
        return lax.rem(spots[u // SIDE][0] + AG_ORDER[u % SIDE], SIDE)

    def forward(u):
        piece = lt_v[u // SIDE].at[chunk_of(u), my_half, :]
        return remote(piece, piece, fw_s.at[u], fw_r.at[u], partner)

    def term(u, accs):
        h, g = u // SIDE, chunk_of(u)
        forward(u).wait()
        left = lt_v[h][g]
        high, mid = halves(left)
        q = jnp.concatenate([high[:RANK], mid[:RANK]], axis=0)
        kv = jnp.concatenate([high[RANK:], mid[RANK:]], axis=0)
        lq[h][g, : 2 * RANK, :] = q
        lq[h][g, 2 * RANK :, :] = q
        tkv[h][g] = jnp.transpose(jnp.concatenate([kv, kv], axis=0))
        return [
            accs[0] + mm_t(fqh[h][g], q),
            accs[1] + mm_t(fqm[h][g], high[:RANK]),
            accs[2] + mm(kv, fkv[h][g]),
        ]

    accs = [
        jnp.zeros((CQ, 2 * RANK), F32),
        jnp.zeros((CQ, RANK), F32),
        jnp.zeros((2 * RANK, 2 * CKV), F32),
    ]

    def pass_on(u):
        h = u // SIDE
        got = rs_buf[h].at[pl.ds(0, SIDE if AG_ORDER[u % SIDE] else SIDE - 1)]
        wait_for(got, ag_r.at[h * SIDE + chunk_of(u)])
        forward(u).start()

    def gram(h):
        return sum(mm_t(lt_v[h][g], lt_v[h][g], precision=HIGHEST) for g in range(SIDE))

    for u in range(SIDE):
        pass_on(u)
    gradient(2, 2, 4)
    for u in range(SIDE):
        accs = term(u, accs)
    for u in range(SIDE, 2 * SIDE):
        pass_on(u)
    early = gram(0)
    for u in range(SIDE, 2 * SIDE):
        accs = term(u, accs)
    pass_on(2 * SIDE)
    pass_on(2 * SIDE + 1)
    accs = term(2 * SIDE, accs)
    pass_on(2 * SIDE + 2)
    accs = term(2 * SIDE + 1, accs)
    pass_on(2 * SIDE + 3)
    accs = term(2 * SIDE + 2, accs)
    accs = term(2 * SIDE + 3, accs)

    by_high = jnp.transpose(accs[0])
    yloc_v[:, CKV:COLS] = by_high[:RANK] + (by_high[RANK:] + jnp.transpose(accs[1]))
    yloc_v[:, :CKV] = accs[2][:RANK, :CKV] + (accs[2][RANK:, :CKV] + accs[2][:RANK, CKV:])
    yloc_v[:, COLS:] = jnp.zeros((RANK, WIDE - COLS), F32)

    my_rows, their_rows = part_of(c, 16), part_of(1 - c, 16)
    cp = remote(yloc_v.at[their_rows, :], yx_v, y_s.at[0], y_r.at[0], partner)
    cp.start()
    cp.wait()
    yz_v[z] = yloc_v[my_rows, :] + yx_v[...]
    for dz in (1, 2, 3):
        remote(yz_v.at[z], yz_v.at[z], y_s.at[1], y_r.at[1], along(0, dz)).start()

    gram_v[:, : 2 * RANK] = early + gram(1) + gram(2)
    gram_v[:, 2 * RANK :] = jnp.zeros((2 * RANK, 2 * RANK), F32)
    row = lax.broadcasted_iota(jnp.int32, (2 * RANK, 128), 0)
    lane = lax.broadcasted_iota(jnp.int32, (2 * RANK, 128), 1)
    same = (row < RANK) == (lane < RANK)
    aug = jnp.where(lane < 2 * RANK, jnp.where(same, gram_v[...], 0.0), jnp.where(lane == row + 2 * RANK, 1.0, 0.0))
    gram_v[:RANK, :] = eliminate(aug[:RANK], 0)
    gram_v[RANK:, :] = eliminate(aug[RANK:], RANK)
    inv = gram_v[:, 2 * RANK :]

    three = yz_v.at[pl.ds(0, 3)]
    wait_for(three, y_r.at[1])
    ysum_v[my_rows, :] = (yz_v[0] + yz_v[1]) + (yz_v[2] + yz_v[3])
    cp = remote(ysum_v.at[my_rows, :], ysum_v.at[my_rows, :], y_s.at[2], y_r.at[2], partner)
    cp.start()
    cp.wait()

    total = ysum_v[...]
    is_kv = lax.broadcasted_iota(jnp.int32, (RANK, WIDE), 1) < CKV
    both = jnp.concatenate([jnp.where(is_kv, 0.0, total), jnp.where(is_kv, total, 0.0)], axis=0)
    new_t = jnp.dot(inv, both, precision=HIGHEST, preferred_element_type=F32) * (1.0 / 8.0)
    factor = tmm(inv, new_t, precision=HIGHEST)
    bn_o[...] = new_t[:RANK] + new_t[RANK:]
    high, mid = halves(factor)
    stack = jnp.concatenate([high[:RANK], high[:RANK], mid[:RANK], mid[:RANK]], axis=0)
    zq_o[...] = jnp.transpose(stack[:, CKV:COLS])
    zkv_o[...] = jnp.concatenate([high[RANK:], high[RANK:], mid[RANK:], mid[RANK:]], axis=0)[:, :CKV]

    for h in range(PARTS):
        wait_for(rs_buf[h], rs_s.at[h])
        wait_for(zbuf[h].at[pl.ds(0, 3)], zs.at[h])
        wait_for(rs_buf[h], ag_s.at[h])
    wait_for(three, y_s.at[1])


def reduce_call(*args):
    any_spec = pl.BlockSpec(memory_space=pl.ANY)
    vmem_spec = pl.BlockSpec(memory_space=pltpu.VMEM)
    dma = pltpu.SemaphoreType.DMA
    v = pltpu.VMEM
    pair = lambda shape, dtype: [v(tuple(w if n is None else n for n in shape), dtype) for w in WIDTHS]
    outs = [
        *pair((SIDE, CQ, None), BF16),
        *pair((SIDE, CQ, None), BF16),
        *pair((SIDE, None, 2 * CKV), BF16),
        *pair((SIDE, 4 * RANK, None), BF16),
        *pair((SIDE, None, 4 * RANK), BF16),
        v((CQ, 4 * RANK), BF16),
        v((4 * RANK, CKV), BF16),
        v((RANK, WIDE), F32),
    ]
    return pl.pallas_call(
        reduce_kernel,
        out_shape=[jax.ShapeDtypeStruct(o.shape, o.dtype) for o in outs],
        in_specs=[any_spec] * 7,
        out_specs=[vmem_spec] * len(outs),
        scratch_shapes=[
            *pair((SIDE, TOK, None), BF16),
            *[v((CQ, SIDE * w), BF16) for w in WIDTHS],
            *[v((SIDE * w, CKV), BF16) for w in WIDTHS],
            *pair((SIDE, 2 * RANK, None), F32),
            *pair((SIDE, RANK, None), F32),
            *pair((SIDE, RANK, None), F32),
            *pair((SIDE * SIDE - 1, 8, None), F32),
            *pair((SIDE, 8, None), F32),
            *pair((SIDE, 2 * RANK, None), F32),
            v((TOK, CKV), BF16),
            v((COLS, TOK), BF16),
            v((RANK, CQ), F32),
            v((RANK, CKV), F32),
            v((4 * RANK, TOK), BF16),
            v((2 * RANK, CQ), BF16),
            v((2 * RANK, CKV), BF16),
            v((RANK, WIDE), F32),
            v((16, WIDE), F32),
            v((SIDE, 16, WIDE), F32),
            v((RANK, WIDE), F32),
            v((2 * RANK, 128), F32),
            dma((4 + 2 * PARTS,)), dma((SIDE * PARTS,)),
            dma((SIDE * PARTS,)), dma((SIDE * PARTS,)),
            dma((PARTS,)), dma((PARTS,)), dma((PARTS,)), dma((PARTS,)),
            dma((PARTS,)), dma((SIDE * PARTS,)), dma((SIDE * PARTS,)), dma((SIDE * PARTS,)),
            dma((3,)), dma((3,)),
        ],
        compiler_params=pltpu.CompilerParams(collective_id=0, has_side_effects=True, vmem_limit_bytes=40 * MIB),
        name="left_and_right_factors",
    )(*[pltpu.with_memory_space_constraint(a, pltpu.HBM) for a in args])


def write_kernel(*refs):
    parts, refs = by_part(refs, 5)
    zq, zkv, bn, uq, ukv, eq, ekv, bq, bkv, *refs = refs
    staged, (sem,) = by_part(refs, 4)
    copies = []
    for h, (fqh, fqm, fkv, lq, tkv, uq_v, ukv_v, eq_v, ekv_v) in enumerate(zip(*parts, *staged)):
        for g in range(SIDE):
            approx = mm(zq[...], lq[g])
            uq_v[g] = approx.astype(BF16)
            eq_v[g] = (fqh[g].astype(F32) + fqm[g].astype(F32) - approx).astype(BF16)
            approx = mm(tkv[g], zkv[...])
            ukv_v[g] = approx.astype(BF16)
            ekv_v[g] = (fkv[g, :, :CKV].astype(F32) + fkv[g, :, CKV:].astype(F32) - approx).astype(BF16)
            at = pl.ds(STARTS[h] + g * WIDTHS[h], WIDTHS[h])
            pairs = [(uq_v, uq.at[:, at]), (ukv_v, ukv.at[at, :]), (eq_v, eq.at[0, :, at]), (ekv_v, ekv.at[0, at, :])]
            for i, (src, dst) in enumerate(pairs):
                cp = pltpu.make_async_copy(src.at[g], dst, sem.at[h * SIDE + g, i])
                cp.start()
                copies.append(cp)
    bkv[...] = bn[:, :CKV]
    bq[...] = bn[:, CKV:COLS]
    for cp in copies:
        cp.wait()


def write_call(*args):
    vmem_spec = pl.BlockSpec(memory_space=pltpu.VMEM)
    any_spec = pl.BlockSpec(memory_space=pl.ANY)
    pair = lambda *shape: [pltpu.VMEM(tuple(w if n is None else n for n in shape), BF16) for w in WIDTHS]
    return pl.pallas_call(
        write_kernel,
        out_shape=[
            jax.ShapeDtypeStruct((CQ, D), BF16),
            jax.ShapeDtypeStruct((D, CKV), BF16),
            jax.ShapeDtypeStruct((1, CQ, D), BF16),
            jax.ShapeDtypeStruct((1, D, CKV), BF16),
            jax.ShapeDtypeStruct((RANK, CQ), F32),
            jax.ShapeDtypeStruct((RANK, CKV), F32),
        ],
        in_specs=[vmem_spec] * len(args),
        out_specs=[any_spec] * 4 + [vmem_spec] * 2,
        scratch_shapes=[
            *pair(SIDE, CQ, None),
            *pair(SIDE, None, CKV),
            *pair(SIDE, CQ, None),
            *pair(SIDE, None, CKV),
            pltpu.SemaphoreType.DMA((SIDE * PARTS, 4)),
        ],
        compiler_params=pltpu.CompilerParams(vmem_limit_bytes=24 * MIB),
        name="updates_and_errors",
    )(*args)


def local(act, ogq, ogkv, eq, ekv, bq, bkv):
    turned = lambda a: jnp.swapaxes(a, -1, -2)
    got = reduce_call(act, turned(ogq), ogkv, turned(eq), ekv, turned(bq), turned(bkv))
    uq, ukv, eq, ekv, bq, bkv = write_call(*got)
    return (turned(uq), ukv, turned(eq), ekv, turned(bq), turned(bkv))


def solution(mesh):
    placed = (
        P("dp", None, None),
        P("dp", None, "tensor"),
        P("dp", None, "tensor"),
        P("dp", None, "tensor"),
        P("dp", None, "tensor"),
        P("tensor", None),
        P("tensor", None),
    )
    return jax.shard_map(
        local,
        mesh=mesh,
        in_specs=placed,
        out_specs=(
            P(None, "tensor"),
            P(None, "tensor"),
            P("dp", None, "tensor"),
            P("dp", None, "tensor"),
            P("tensor", None),
            P("tensor", None),
        ),
        check_vma=False,
    )
```

```python
import functools

import jax
import jax.numpy as jnp
from jax import lax
from jax.experimental import pallas as pl
from jax.experimental.pallas import tpu as pltpu
from jax.sharding import PartitionSpec as P

F32 = jnp.float32
BF16 = jnp.bfloat16
MESH = pl.DeviceIdType.MESH
HIGHEST = lax.Precision.HIGHEST
MIB = 1 << 20

SIDE = 4
D = 5120
WIDTHS = (512, 384, 384)
PARTS = len(WIDTHS)
STARTS = tuple(SIDE * sum(WIDTHS[:h]) for h in range(PARTS))
TOK = 1024
CQ, CKV = 320, 128
COLS = CQ + CKV
RANK = 32
WIDE = 512
ROT = (1, 3, 2, 0)
AG_ORDER = (0, 1, 3, 2)
AHEAD = 3
GATE = 4
LAG = 2
UNITS = [(h, k) for h in range(PARTS) for k in range(SIDE)]


def mm(a, b):
    return jnp.dot(a, b, preferred_element_type=F32)


def mm_t(a, b, precision=None):
    return lax.dot_general(a, b, (((1,), (1,)), ((), ())), preferred_element_type=F32, precision=precision)


def tmm(a, b, precision=None):
    return lax.dot_general(a, b, (((0,), (0,)), ((), ())), preferred_element_type=F32, precision=precision)


def halves(v):
    high = v.astype(BF16)
    return high, (v - high.astype(F32)).astype(BF16)


def eliminate(a, off):
    row = lax.broadcasted_iota(jnp.int32, (RANK, 128), 0)
    lane = lax.broadcasted_iota(jnp.int32, (RANK, 128), 1)
    for k in range(RANK - 1):
        col = jnp.broadcast_to(a[:, off + k : off + k + 1], (RANK, 128))
        scaled = a[k : k + 1, :] / col[k : k + 1, :]
        a = a - jnp.where(row > k, col, 0.0) * scaled
    diag = jnp.sum(jnp.where(lane == row + off, a, 0.0), axis=1, keepdims=True)
    return a * lax.rsqrt(diag)


def by_part(refs, count):
    return [refs[i * PARTS : (i + 1) * PARTS] for i in range(count)], refs[count * PARTS :]


def reduce_kernel(act, ogq, ogkv, eq, ekv, bq, bkv, *refs):
    (fqh, fqm, fkv, lq, tkv), refs = by_part(refs, 5)
    zq_o, zkv_o, bn_o, *refs = refs
    (act_v, eq_v, ekv_v, loc_v, xr_v, sum_v, rs_buf, zbuf, lt_v), refs = by_part(refs, 9)
    ogkv_v, og_v, bq_v, bkv_v, pst_v, bq2_v, bkv2_v, yloc_v, yx_v, yz_v, ysum_v, gram_v, *refs = refs
    ld, lda, xs, xr, rs_s, rs_r, zs, zr, ag_s, ag_r, fw_s, fw_r, y_s, y_r = refs

    dp, t = lax.axis_index("dp"), lax.axis_index("tensor")
    z, c = dp // 2, lax.rem(dp, 2)
    x, y = t // SIDE, lax.rem(t, SIDE)
    partner = (z * 2 + 1 - c, t)

    spots = ((x, y, z), (y, z, x), (z, x, y))

    def moved(d):
        return (lax.rem(z + d[2], SIDE) * 2 + c, lax.rem(x + d[0], SIDE) * SIDE + lax.rem(y + d[1], SIDE))

    def plane(h, d1, d2):
        return moved(((d1, d2, 0), (0, d1, d2), (d2, 0, d1))[h])

    def along(h, d):
        return moved(((0, 0, d), (d, 0, 0), (0, d, 0))[h])

    def part_of(rows, size):
        return pl.ds(pl.multiple_of(rows * size, size), size)

    def remote(src, dst, send, recv, device):
        return pltpu.make_async_remote_copy(
            src_ref=src, dst_ref=dst, send_sem=send, recv_sem=recv, device_id=device, device_id_type=MESH
        )

    def wait_for(ref, sem):
        pltpu.make_async_copy(ref, ref, sem).wait()

    def load(u):
        h, k = UNITS[u]
        g = lax.rem(spots[h][0] + ROT[k], SIDE)
        at = pl.ds(pl.multiple_of(STARTS[h] + g * WIDTHS[h], 128), WIDTHS[h])
        return pltpu.make_async_copy(act.at[0, :, at], act_v[h].at[g], lda.at[u])

    def load_errors(h):
        at = pl.ds(STARTS[h], SIDE * WIDTHS[h])
        return [
            pltpu.make_async_copy(eq.at[0, :, at], eq_v[h], ld.at[4 + 2 * h]),
            pltpu.make_async_copy(ekv.at[0, at, :], ekv_v[h], ld.at[5 + 2 * h]),
        ]

    first = [
        pltpu.make_async_copy(src, dst, ld.at[i])
        for i, (src, dst) in enumerate(
            [(ogq.at[0], og_v.at[pl.ds(CKV, CQ), :]), (ogkv.at[0], ogkv_v), (bq, bq_v), (bkv, bkv_v)]
        )
    ]
    for cp in first + load_errors(0) + [load(u) for u in range(AHEAD)]:
        cp.start()

    barrier = pltpu.get_barrier_semaphore()
    peers = [partner]
    peers += [moved((i, j, 0)) for i in range(SIDE) for j in range(SIDE) if i or j]
    peers += [moved((i, 0, j)) for i in range(SIDE) for j in (1, 2, 3)]
    peers += [moved((0, i, j)) for i in (1, 2, 3) for j in (1, 2, 3)]
    for p in peers:
        pl.semaphore_signal(barrier, inc=1, device_id=p, device_id_type=MESH)

    for cp in first:
        cp.wait()
    og_v[:CKV, :] = jnp.transpose(ogkv_v[...])
    for src, b2, og_rows, base in ((bq_v, bq2_v, slice(CKV, COLS), 0), (bkv_v, bkv2_v, slice(0, CKV), 2 * RANK)):
        bt = src[...]
        high, mid = halves(bt)
        low = (bt - high.astype(F32) - mid.astype(F32)).astype(BF16)
        b2[:RANK, :] = high
        b2[RANK:, :] = mid
        og_w = og_v[og_rows, :]
        proj = mm(high, og_w) + (mm(mid, og_w) + mm(low, og_w))
        p_high, p_mid = halves(proj)
        pst_v[base : base + RANK, :] = p_high
        pst_v[base + RANK : base + 2 * RANK, :] = p_mid

    my_half, their_half = part_of(c, RANK), part_of(1 - c, RANK)

    def exchange(u):
        h, k = UNITS[u]
        return remote(loc_v[h].at[k, their_half, :], xr_v[h].at[k], xs.at[u], xr.at[u], partner)

    def scatter(u):
        h, k = UNITS[u]
        exchange(u).wait()
        sum_v[h][k] = loc_v[h][k, my_half, :] + xr_v[h][k]
        for dy in range(SIDE):
            if ROT[k] or dy:
                rows = part_of(lax.rem(spots[h][1] + dy, SIDE), 8)
                remote(
                    sum_v[h].at[k, rows, :], rs_buf[h].at[ROT[k] * SIDE + dy - 1], rs_s.at[h], rs_r.at[h],
                    plane(h, ROT[k], dy),
                ).start()

    for u, (h, k) in enumerate(UNITS):
        g = lax.rem(spots[h][0] + ROT[k], SIDE)
        load(u).wait()
        if k == 0:
            for cp in load_errors(h):
                cp.wait()
        if k == 1 and h + 1 < PARTS:
            for cp in load_errors(h + 1):
                cp.start()
        for later in range(u + AHEAD, min(u + AHEAD + 1, len(UNITS)) if u < GATE else len(UNITS) if u == GATE else 0):
            load(later).start()
        bq2, bkv2 = bq2_v[...], bkv2_v[...]
        pst = pst_v[...]
        at = pl.ds(pl.multiple_of(g * WIDTHS[h], 128), WIDTHS[h])
        prod = mm(pst, act_v[h][g])
        from_q = mm(bq2, eq_v[h][:, at])
        from_kv = mm_t(bkv2, ekv_v[h][at, :])
        loc_v[h][k, :RANK, :] = (prod[:RANK] + prod[RANK : 2 * RANK]) + (from_q[:RANK] + from_q[RANK:])
        loc_v[h][k, RANK:, :] = (prod[2 * RANK : 3 * RANK] + prod[3 * RANK :]) + (from_kv[:RANK] + from_kv[RANK:])
        if u == GATE:
            pl.semaphore_wait(barrier, len(peers))
            for v in range(GATE):
                exchange(v).start()
        if u >= GATE:
            exchange(u).start()
        if u > GATE:
            for v in range(max(0, u - LAG) if u > GATE + 1 else 0, u - LAG + 1):
                scatter(v)
    for v in range(len(UNITS) - LAG, len(UNITS)):
        scatter(v)

    def gradient(h, lo, hi):
        width = WIDTHS[h]

        def body(g, _):
            at = pl.ds(pl.multiple_of(g * width, width), width)
            grads = mm(og_v[...], act_v[h][g])
            high, mid = halves(jnp.transpose(grads[:CKV]) + ekv_v[h][at, :].astype(F32))
            fkv[h][g, :, :CKV] = high
            fkv[h][g, :, CKV:] = mid
            high, mid = halves(grads[CKV:] + eq_v[h][:, at].astype(F32))
            fqh[h][g] = high
            fqm[h][g] = mid
            return 0

        lax.fori_loop(lo, hi, body, 0)

    def sum_plane(h):
        wait_for(rs_buf[h], rs_r.at[h])
        part = sum_v[h][SIDE - 1, part_of(spots[h][1], 8), :]
        for o in range(SIDE * SIDE - 1):
            part = part + rs_buf[h][o]
        here = spots[h][2]
        zbuf[h][here] = part
        for d in (1, 2, 3):
            remote(zbuf[h].at[here], zbuf[h].at[here], zs.at[h], zr.at[h], along(h, d)).start()

    def gather(h):
        wait_for(zbuf[h].at[pl.ds(0, 3)], zr.at[h])
        g, own = spots[h][0], part_of(c * SIDE + spots[h][1], 8)
        lt_v[h][g, own, :] = (zbuf[h][0] + zbuf[h][1]) + (zbuf[h][2] + zbuf[h][3])
        for d1 in AG_ORDER:
            for d2 in range(SIDE):
                if d1 or d2:
                    piece = lt_v[h].at[g, own, :]
                    remote(piece, piece, ag_s.at[h], ag_r.at[h * SIDE + g], plane(h, d1, d2)).start()

    gradient(0, 0, 2)
    sum_plane(0)
    gradient(0, 2, 3)
    sum_plane(1)
    gradient(0, 3, 4)
    gather(0)
    sum_plane(2)
    gradient(1, 0, 2)
    gather(1)
    gradient(1, 2, 4)
    gather(2)
    gradient(2, 0, 2)

    def chunk_of(u):
        return lax.rem(spots[u // SIDE][0] + AG_ORDER[u % SIDE], SIDE)

    def forward(u):
        piece = lt_v[u // SIDE].at[chunk_of(u), my_half, :]
        return remote(piece, piece, fw_s.at[u], fw_r.at[u], partner)

    def term(u, accs):
        h, g = u // SIDE, chunk_of(u)
        forward(u).wait()
        left = lt_v[h][g]
        high, mid = halves(left)
        q = jnp.concatenate([high[:RANK], mid[:RANK]], axis=0)
        kv = jnp.concatenate([high[RANK:], mid[RANK:]], axis=0)
        lq[h][g, : 2 * RANK, :] = q
        lq[h][g, 2 * RANK :, :] = q
        tkv[h][g] = jnp.transpose(jnp.concatenate([kv, kv], axis=0))
        return [
            accs[0] + mm_t(fqh[h][g], q),
            accs[1] + mm_t(fqm[h][g], high[:RANK]),
            accs[2] + mm(kv, fkv[h][g]),
        ]

    accs = [
        jnp.zeros((CQ, 2 * RANK), F32),
        jnp.zeros((CQ, RANK), F32),
        jnp.zeros((2 * RANK, 2 * CKV), F32),
    ]

    def pass_on(u):
        h = u // SIDE
        got = rs_buf[h].at[pl.ds(0, SIDE if AG_ORDER[u % SIDE] else SIDE - 1)]
        wait_for(got, ag_r.at[h * SIDE + chunk_of(u)])
        forward(u).start()

    def gram(h):
        return sum(mm_t(lt_v[h][g], lt_v[h][g], precision=HIGHEST) for g in range(SIDE))

    for u in range(SIDE):
        pass_on(u)
    gradient(2, 2, 4)
    for u in range(SIDE):
        accs = term(u, accs)
    for u in range(SIDE, 2 * SIDE):
        pass_on(u)
    early = gram(0)
    for u in range(SIDE, 2 * SIDE):
        accs = term(u, accs)
    for u in range(2 * SIDE, 3 * SIDE):
        pass_on(u)
    for u in range(2 * SIDE, 3 * SIDE):
        accs = term(u, accs)

    by_high = jnp.transpose(accs[0])
    yloc_v[:, CKV:COLS] = by_high[:RANK] + (by_high[RANK:] + jnp.transpose(accs[1]))
    yloc_v[:, :CKV] = accs[2][:RANK, :CKV] + (accs[2][RANK:, :CKV] + accs[2][:RANK, CKV:])
    yloc_v[:, COLS:] = jnp.zeros((RANK, WIDE - COLS), F32)

    my_rows, their_rows = part_of(c, 16), part_of(1 - c, 16)
    cp = remote(yloc_v.at[their_rows, :], yx_v, y_s.at[0], y_r.at[0], partner)
    cp.start()
    cp.wait()
    yz_v[z] = yloc_v[my_rows, :] + yx_v[...]
    for dz in (1, 2, 3):
        remote(yz_v.at[z], yz_v.at[z], y_s.at[1], y_r.at[1], along(0, dz)).start()

    gram_v[:, : 2 * RANK] = early + gram(1) + gram(2)
    gram_v[:, 2 * RANK :] = jnp.zeros((2 * RANK, 2 * RANK), F32)
    row = lax.broadcasted_iota(jnp.int32, (2 * RANK, 128), 0)
    lane = lax.broadcasted_iota(jnp.int32, (2 * RANK, 128), 1)
    same = (row < RANK) == (lane < RANK)
    aug = jnp.where(lane < 2 * RANK, jnp.where(same, gram_v[...], 0.0), jnp.where(lane == row + 2 * RANK, 1.0, 0.0))
    gram_v[:RANK, :] = eliminate(aug[:RANK], 0)
    gram_v[RANK:, :] = eliminate(aug[RANK:], RANK)
    inv = gram_v[:, 2 * RANK :]

    three = yz_v.at[pl.ds(0, 3)]
    wait_for(three, y_r.at[1])
    ysum_v[my_rows, :] = (yz_v[0] + yz_v[1]) + (yz_v[2] + yz_v[3])
    cp = remote(ysum_v.at[my_rows, :], ysum_v.at[my_rows, :], y_s.at[2], y_r.at[2], partner)
    cp.start()
    cp.wait()

    total = ysum_v[...]
    is_kv = lax.broadcasted_iota(jnp.int32, (RANK, WIDE), 1) < CKV
    both = jnp.concatenate([jnp.where(is_kv, 0.0, total), jnp.where(is_kv, total, 0.0)], axis=0)
    new_t = jnp.dot(inv, both, precision=HIGHEST, preferred_element_type=F32) * (1.0 / 8.0)
    factor = tmm(inv, new_t, precision=HIGHEST)
    bn_o[...] = new_t[:RANK] + new_t[RANK:]
    high, mid = halves(factor)
    stack = jnp.concatenate([high[:RANK], high[:RANK], mid[:RANK], mid[:RANK]], axis=0)
    zq_o[...] = jnp.transpose(stack[:, CKV:COLS])
    zkv_o[...] = jnp.concatenate([high[RANK:], high[RANK:], mid[RANK:], mid[RANK:]], axis=0)[:, :CKV]

    for h in range(PARTS):
        wait_for(rs_buf[h], rs_s.at[h])
        wait_for(zbuf[h].at[pl.ds(0, 3)], zs.at[h])
        wait_for(rs_buf[h], ag_s.at[h])
    wait_for(three, y_s.at[1])


def reduce_call(*args):
    any_spec = pl.BlockSpec(memory_space=pl.ANY)
    vmem_spec = pl.BlockSpec(memory_space=pltpu.VMEM)
    dma = pltpu.SemaphoreType.DMA
    v = pltpu.VMEM
    pair = lambda shape, dtype: [v(tuple(w if n is None else n for n in shape), dtype) for w in WIDTHS]
    outs = [
        *pair((SIDE, CQ, None), BF16),
        *pair((SIDE, CQ, None), BF16),
        *pair((SIDE, None, 2 * CKV), BF16),
        *pair((SIDE, 4 * RANK, None), BF16),
        *pair((SIDE, None, 4 * RANK), BF16),
        v((CQ, 4 * RANK), BF16),
        v((4 * RANK, CKV), BF16),
        v((RANK, WIDE), F32),
    ]
    return pl.pallas_call(
        reduce_kernel,
        out_shape=[jax.ShapeDtypeStruct(o.shape, o.dtype) for o in outs],
        in_specs=[any_spec] * 7,
        out_specs=[vmem_spec] * len(outs),
        scratch_shapes=[
            *pair((SIDE, TOK, None), BF16),
            *[v((CQ, SIDE * w), BF16) for w in WIDTHS],
            *[v((SIDE * w, CKV), BF16) for w in WIDTHS],
            *pair((SIDE, 2 * RANK, None), F32),
            *pair((SIDE, RANK, None), F32),
            *pair((SIDE, RANK, None), F32),
            *pair((SIDE * SIDE - 1, 8, None), F32),
            *pair((SIDE, 8, None), F32),
            *pair((SIDE, 2 * RANK, None), F32),
            v((TOK, CKV), BF16),
            v((COLS, TOK), BF16),
            v((RANK, CQ), F32),
            v((RANK, CKV), F32),
            v((4 * RANK, TOK), BF16),
            v((2 * RANK, CQ), BF16),
            v((2 * RANK, CKV), BF16),
            v((RANK, WIDE), F32),
            v((16, WIDE), F32),
            v((SIDE, 16, WIDE), F32),
            v((RANK, WIDE), F32),
            v((2 * RANK, 128), F32),
            dma((4 + 2 * PARTS,)), dma((SIDE * PARTS,)),
            dma((SIDE * PARTS,)), dma((SIDE * PARTS,)),
            dma((PARTS,)), dma((PARTS,)), dma((PARTS,)), dma((PARTS,)),
            dma((PARTS,)), dma((SIDE * PARTS,)), dma((SIDE * PARTS,)), dma((SIDE * PARTS,)),
            dma((3,)), dma((3,)),
        ],
        compiler_params=pltpu.CompilerParams(collective_id=0, has_side_effects=True, vmem_limit_bytes=40 * MIB),
        name="left_and_right_factors",
    )(*[pltpu.with_memory_space_constraint(a, pltpu.HBM) for a in args])


def write_kernel(*refs):
    parts, refs = by_part(refs, 5)
    zq, zkv, bn, uq, ukv, eq, ekv, bq, bkv, *refs = refs
    staged, (sem,) = by_part(refs, 4)
    copies = []
    for h, (fqh, fqm, fkv, lq, tkv, uq_v, ukv_v, eq_v, ekv_v) in enumerate(zip(*parts, *staged)):
        for g in range(SIDE):
            approx = mm(zq[...], lq[g])
            uq_v[g] = approx.astype(BF16)
            eq_v[g] = (fqh[g].astype(F32) + fqm[g].astype(F32) - approx).astype(BF16)
            approx = mm(tkv[g], zkv[...])
            ukv_v[g] = approx.astype(BF16)
            ekv_v[g] = (fkv[g, :, :CKV].astype(F32) + fkv[g, :, CKV:].astype(F32) - approx).astype(BF16)
            at = pl.ds(STARTS[h] + g * WIDTHS[h], WIDTHS[h])
            pairs = [(uq_v, uq.at[:, at]), (ukv_v, ukv.at[at, :]), (eq_v, eq.at[0, :, at]), (ekv_v, ekv.at[0, at, :])]
            for i, (src, dst) in enumerate(pairs):
                cp = pltpu.make_async_copy(src.at[g], dst, sem.at[h * SIDE + g, i])
                cp.start()
                copies.append(cp)
    bkv[...] = bn[:, :CKV]
    bq[...] = bn[:, CKV:COLS]
    for cp in copies:
        cp.wait()


def write_call(*args):
    vmem_spec = pl.BlockSpec(memory_space=pltpu.VMEM)
    any_spec = pl.BlockSpec(memory_space=pl.ANY)
    pair = lambda *shape: [pltpu.VMEM(tuple(w if n is None else n for n in shape), BF16) for w in WIDTHS]
    return pl.pallas_call(
        write_kernel,
        out_shape=[
            jax.ShapeDtypeStruct((CQ, D), BF16),
            jax.ShapeDtypeStruct((D, CKV), BF16),
            jax.ShapeDtypeStruct((1, CQ, D), BF16),
            jax.ShapeDtypeStruct((1, D, CKV), BF16),
            jax.ShapeDtypeStruct((RANK, CQ), F32),
            jax.ShapeDtypeStruct((RANK, CKV), F32),
        ],
        in_specs=[vmem_spec] * len(args),
        out_specs=[any_spec] * 4 + [vmem_spec] * 2,
        scratch_shapes=[
            *pair(SIDE, CQ, None),
            *pair(SIDE, None, CKV),
            *pair(SIDE, CQ, None),
            *pair(SIDE, None, CKV),
            pltpu.SemaphoreType.DMA((SIDE * PARTS, 4)),
        ],
        compiler_params=pltpu.CompilerParams(vmem_limit_bytes=24 * MIB),
        name="updates_and_errors",
    )(*args)


def local(act, ogq, ogkv, eq, ekv, bq, bkv):
    turned = lambda a: jnp.swapaxes(a, -1, -2)
    got = reduce_call(act, turned(ogq), ogkv, turned(eq), ekv, turned(bq), turned(bkv))
    uq, ukv, eq, ekv, bq, bkv = write_call(*got)
    return (turned(uq), ukv, turned(eq), ekv, turned(bq), turned(bkv))


def solution(mesh):
    placed = (
        P("dp", None, None),
        P("dp", None, "tensor"),
        P("dp", None, "tensor"),
        P("dp", None, "tensor"),
        P("dp", None, "tensor"),
        P("tensor", None),
        P("tensor", None),
    )
    return jax.shard_map(
        local,
        mesh=mesh,
        in_specs=placed,
        out_specs=(
            P(None, "tensor"),
            P(None, "tensor"),
            P("dp", None, "tensor"),
            P("dp", None, "tensor"),
            P("tensor", None),
            P("tensor", None),
        ),
        check_vma=False,
    )
```

```python
import functools

import jax
import jax.numpy as jnp
from jax import lax
from jax.experimental import pallas as pl
from jax.experimental.pallas import tpu as pltpu
from jax.sharding import PartitionSpec as P

F32 = jnp.float32
BF16 = jnp.bfloat16
MESH = pl.DeviceIdType.MESH
HIGHEST = lax.Precision.HIGHEST
MIB = 1 << 20

SIDE = 4
D = 5120
WIDTHS = (512, 384, 384)
PARTS = len(WIDTHS)
STARTS = tuple(SIDE * sum(WIDTHS[:h]) for h in range(PARTS))
TOK = 1024
CQ, CKV = 320, 128
COLS = CQ + CKV
RANK = 32
WIDE = 512
ROT = (1, 3, 2, 0)
AG_ORDER = (0, 1, 3, 2)
AHEAD = 3
GATE = 4
LAG = 2
UNITS = [(h, k) for h in range(PARTS) for k in range(SIDE)]


def mm(a, b):
    return jnp.dot(a, b, preferred_element_type=F32)


def mm_t(a, b, precision=None):
    return lax.dot_general(a, b, (((1,), (1,)), ((), ())), preferred_element_type=F32, precision=precision)


def tmm(a, b, precision=None):
    return lax.dot_general(a, b, (((0,), (0,)), ((), ())), preferred_element_type=F32, precision=precision)


def halves(v):
    high = v.astype(BF16)
    return high, (v - high.astype(F32)).astype(BF16)


def eliminate(a, off):
    row = lax.broadcasted_iota(jnp.int32, (RANK, 128), 0)
    lane = lax.broadcasted_iota(jnp.int32, (RANK, 128), 1)
    for k in range(RANK - 1):
        col = jnp.broadcast_to(a[:, off + k : off + k + 1], (RANK, 128))
        scaled = a[k : k + 1, :] / col[k : k + 1, :]
        a = a - jnp.where(row > k, col, 0.0) * scaled
    diag = jnp.sum(jnp.where(lane == row + off, a, 0.0), axis=1, keepdims=True)
    return a * lax.rsqrt(diag)


def by_part(refs, count):
    return [refs[i * PARTS : (i + 1) * PARTS] for i in range(count)], refs[count * PARTS :]


def reduce_kernel(act, ogq, ogkv, eq, ekv, bq, bkv, *refs):
    (fqh, fqm, fkv, lq, tkv), refs = by_part(refs, 5)
    zq_o, zkv_o, bn_o, *refs = refs
    (act_v, eq_v, ekv_v, loc_v, xr_v, sum_v, rs_buf, zbuf, lt_v), refs = by_part(refs, 9)
    ogkv_v, og_v, bq_v, bkv_v, pst_v, bq2_v, bkv2_v, yloc_v, yx_v, yz_v, ysum_v, gram_v, *refs = refs
    ld, lda, xs, xr, rs_s, rs_r, zs, zr, ag_s, ag_r, fw_s, fw_r, y_s, y_r = refs

    dp, t = lax.axis_index("dp"), lax.axis_index("tensor")
    z, c = dp // 2, lax.rem(dp, 2)
    x, y = t // SIDE, lax.rem(t, SIDE)
    partner = (z * 2 + 1 - c, t)

    spots = ((x, y, z), (y, z, x), (z, x, y))

    def moved(d):
        return (lax.rem(z + d[2], SIDE) * 2 + c, lax.rem(x + d[0], SIDE) * SIDE + lax.rem(y + d[1], SIDE))

    def plane(h, d1, d2):
        return moved(((d1, d2, 0), (0, d1, d2), (d2, 0, d1))[h])

    def along(h, d):
        return moved(((0, 0, d), (d, 0, 0), (0, d, 0))[h])

    def part_of(rows, size):
        return pl.ds(pl.multiple_of(rows * size, size), size)

    def remote(src, dst, send, recv, device):
        return pltpu.make_async_remote_copy(
            src_ref=src, dst_ref=dst, send_sem=send, recv_sem=recv, device_id=device, device_id_type=MESH
        )

    def wait_for(ref, sem):
        pltpu.make_async_copy(ref, ref, sem).wait()

    def load(u):
        h, k = UNITS[u]
        g = lax.rem(spots[h][0] + ROT[k], SIDE)
        at = pl.ds(pl.multiple_of(STARTS[h] + g * WIDTHS[h], 128), WIDTHS[h])
        return pltpu.make_async_copy(act.at[0, :, at], act_v[h].at[g], lda.at[u])

    def load_errors(h):
        at = pl.ds(STARTS[h], SIDE * WIDTHS[h])
        return [
            pltpu.make_async_copy(eq.at[0, :, at], eq_v[h], ld.at[4 + 2 * h]),
            pltpu.make_async_copy(ekv.at[0, at, :], ekv_v[h], ld.at[5 + 2 * h]),
        ]

    first = [
        pltpu.make_async_copy(src, dst, ld.at[i])
        for i, (src, dst) in enumerate(
            [(ogq.at[0], og_v.at[pl.ds(CKV, CQ), :]), (ogkv.at[0], ogkv_v), (bq, bq_v), (bkv, bkv_v)]
        )
    ]
    for cp in first + load_errors(0) + [load(u) for u in range(AHEAD)]:
        cp.start()

    barrier = pltpu.get_barrier_semaphore()
    peers = [partner]
    offsets = [(i, j, 0) for i in range(SIDE) for j in range(SIDE) if i or j]
    offsets += [(i, 0, j) for i in range(SIDE) for j in (1, 2, 3)]
    offsets += [(0, i, j) for i in (1, 2, 3) for j in (1, 2, 3)]
    peers += [moved(d) for d in sorted(offsets, key=lambda d: sum(min(i, SIDE - i) for i in d))]
    for p in reversed(peers):
        pl.semaphore_signal(barrier, inc=1, device_id=p, device_id_type=MESH)

    for cp in first:
        cp.wait()
    og_v[:CKV, :] = jnp.transpose(ogkv_v[...])
    for src, b2, og_rows, base in ((bq_v, bq2_v, slice(CKV, COLS), 0), (bkv_v, bkv2_v, slice(0, CKV), 2 * RANK)):
        bt = src[...]
        high, mid = halves(bt)
        low = (bt - high.astype(F32) - mid.astype(F32)).astype(BF16)
        b2[:RANK, :] = high
        b2[RANK:, :] = mid
        og_w = og_v[og_rows, :]
        proj = mm(high, og_w) + (mm(mid, og_w) + mm(low, og_w))
        p_high, p_mid = halves(proj)
        pst_v[base : base + RANK, :] = p_high
        pst_v[base + RANK : base + 2 * RANK, :] = p_mid

    my_half, their_half = part_of(c, RANK), part_of(1 - c, RANK)

    def exchange(u):
        h, k = UNITS[u]
        return remote(loc_v[h].at[k, their_half, :], xr_v[h].at[k], xs.at[u], xr.at[u], partner)

    def scatter(u):
        h, k = UNITS[u]
        exchange(u).wait()
        sum_v[h][k] = loc_v[h][k, my_half, :] + xr_v[h][k]
        for dy in range(SIDE):
            if ROT[k] or dy:
                rows = part_of(lax.rem(spots[h][1] + dy, SIDE), 8)
                remote(
                    sum_v[h].at[k, rows, :], rs_buf[h].at[ROT[k] * SIDE + dy - 1], rs_s.at[h], rs_r.at[h],
                    plane(h, ROT[k], dy),
                ).start()

    for u, (h, k) in enumerate(UNITS):
        g = lax.rem(spots[h][0] + ROT[k], SIDE)
        load(u).wait()
        if k == 0:
            for cp in load_errors(h):
                cp.wait()
        if k == 1 and h + 1 < PARTS:
            for cp in load_errors(h + 1):
                cp.start()
        for later in range(u + AHEAD, min(u + AHEAD + 1, len(UNITS)) if u < GATE else len(UNITS) if u == GATE else 0):
            load(later).start()
        bq2, bkv2 = bq2_v[...], bkv2_v[...]
        pst = pst_v[...]
        at = pl.ds(pl.multiple_of(g * WIDTHS[h], 128), WIDTHS[h])
        prod = mm(pst, act_v[h][g])
        from_q = mm(bq2, eq_v[h][:, at])
        from_kv = mm_t(bkv2, ekv_v[h][at, :])
        loc_v[h][k, :RANK, :] = (prod[:RANK] + prod[RANK : 2 * RANK]) + (from_q[:RANK] + from_q[RANK:])
        loc_v[h][k, RANK:, :] = (prod[2 * RANK : 3 * RANK] + prod[3 * RANK :]) + (from_kv[:RANK] + from_kv[RANK:])
        if u == GATE:
            pl.semaphore_wait(barrier, len(peers))
            for v in range(GATE):
                exchange(v).start()
        if u >= GATE:
            exchange(u).start()
        if u > GATE:
            for v in range(max(0, u - LAG) if u > GATE + 1 else 0, u - LAG + 1):
                scatter(v)
    for v in range(len(UNITS) - LAG, len(UNITS)):
        scatter(v)

    def gradient(h, lo, hi):
        width = WIDTHS[h]

        def body(g, _):
            at = pl.ds(pl.multiple_of(g * width, width), width)
            grads = mm(og_v[...], act_v[h][g])
            high, mid = halves(jnp.transpose(grads[:CKV]) + ekv_v[h][at, :].astype(F32))
            fkv[h][g, :, :CKV] = high
            fkv[h][g, :, CKV:] = mid
            high, mid = halves(grads[CKV:] + eq_v[h][:, at].astype(F32))
            fqh[h][g] = high
            fqm[h][g] = mid
            return 0

        lax.fori_loop(lo, hi, body, 0)

    def sum_plane(h):
        wait_for(rs_buf[h], rs_r.at[h])
        part = sum_v[h][SIDE - 1, part_of(spots[h][1], 8), :]
        for o in range(SIDE * SIDE - 1):
            part = part + rs_buf[h][o]
        here = spots[h][2]
        zbuf[h][here] = part
        for d in (1, 2, 3):
            remote(zbuf[h].at[here], zbuf[h].at[here], zs.at[h], zr.at[h], along(h, d)).start()

    def gather(h):
        wait_for(zbuf[h].at[pl.ds(0, 3)], zr.at[h])
        g, own = spots[h][0], part_of(c * SIDE + spots[h][1], 8)
        lt_v[h][g, own, :] = (zbuf[h][0] + zbuf[h][1]) + (zbuf[h][2] + zbuf[h][3])
        for d1 in AG_ORDER:
            for d2 in range(SIDE):
                if d1 or d2:
                    piece = lt_v[h].at[g, own, :]
                    remote(piece, piece, ag_s.at[h], ag_r.at[h * SIDE + g], plane(h, d1, d2)).start()

    gradient(0, 0, 2)
    sum_plane(0)
    gradient(0, 2, 3)
    sum_plane(1)
    gradient(0, 3, 4)
    gather(0)
    sum_plane(2)
    gradient(1, 0, 2)
    gather(1)
    gradient(1, 2, 4)
    gather(2)
    gradient(2, 0, 2)

    def chunk_of(u):
        return lax.rem(spots[u // SIDE][0] + AG_ORDER[u % SIDE], SIDE)

    def forward(u):
        piece = lt_v[u // SIDE].at[chunk_of(u), my_half, :]
        return remote(piece, piece, fw_s.at[u], fw_r.at[u], partner)

    def split_left(h, g):
        high, mid = halves(lt_v[h][g])
        q = jnp.concatenate([high[:RANK], mid[:RANK]], axis=0)
        return high, q, jnp.concatenate([high[RANK:], mid[RANK:]], axis=0)

    def hand_over(h, g, q, kv):
        lq[h][g, : 2 * RANK, :] = q
        lq[h][g, 2 * RANK :, :] = q
        tkv[h][g] = jnp.transpose(jnp.concatenate([kv, kv], axis=0))

    def term(u, accs):
        h, g = u // SIDE, chunk_of(u)
        forward(u).wait()
        high, q, kv = split_left(h, g)
        if h < PARTS - 1:
            hand_over(h, g, q, kv)
        return [
            accs[0] + mm_t(fqh[h][g], q),
            accs[1] + mm_t(fqm[h][g], high[:RANK]),
            accs[2] + mm(kv, fkv[h][g]),
        ]

    accs = [
        jnp.zeros((CQ, 2 * RANK), F32),
        jnp.zeros((CQ, RANK), F32),
        jnp.zeros((2 * RANK, 2 * CKV), F32),
    ]

    def pass_on(u):
        h = u // SIDE
        got = rs_buf[h].at[pl.ds(0, SIDE if AG_ORDER[u % SIDE] else SIDE - 1)]
        wait_for(got, ag_r.at[h * SIDE + chunk_of(u)])
        forward(u).start()

    def gram(h):
        return sum(mm_t(lt_v[h][g], lt_v[h][g], precision=HIGHEST) for g in range(SIDE))

    for u in range(SIDE):
        pass_on(u)
    gradient(2, 2, 4)
    for u in range(SIDE):
        accs = term(u, accs)
    for u in range(SIDE, 2 * SIDE):
        pass_on(u)
    early = gram(0)
    for u in range(SIDE, 2 * SIDE):
        accs = term(u, accs)
    for u in range(2 * SIDE, 3 * SIDE):
        pass_on(u)
    for u in range(2 * SIDE, 3 * SIDE):
        accs = term(u, accs)

    by_high = jnp.transpose(accs[0])
    yloc_v[:, CKV:COLS] = by_high[:RANK] + (by_high[RANK:] + jnp.transpose(accs[1]))
    yloc_v[:, :CKV] = accs[2][:RANK, :CKV] + (accs[2][RANK:, :CKV] + accs[2][:RANK, CKV:])
    yloc_v[:, COLS:] = jnp.zeros((RANK, WIDE - COLS), F32)

    my_rows, their_rows = part_of(c, 16), part_of(1 - c, 16)
    cp = remote(yloc_v.at[their_rows, :], yx_v, y_s.at[0], y_r.at[0], partner)
    cp.start()
    cp.wait()
    yz_v[z] = yloc_v[my_rows, :] + yx_v[...]
    for dz in (1, 2, 3):
        remote(yz_v.at[z], yz_v.at[z], y_s.at[1], y_r.at[1], along(0, dz)).start()

    for g in range(SIDE):
        hand_over(PARTS - 1, g, *split_left(PARTS - 1, g)[1:])
    gram_v[:, : 2 * RANK] = early + gram(1) + gram(2)
    gram_v[:, 2 * RANK :] = jnp.zeros((2 * RANK, 2 * RANK), F32)
    row = lax.broadcasted_iota(jnp.int32, (2 * RANK, 128), 0)
    lane = lax.broadcasted_iota(jnp.int32, (2 * RANK, 128), 1)
    same = (row < RANK) == (lane < RANK)
    aug = jnp.where(lane < 2 * RANK, jnp.where(same, gram_v[...], 0.0), jnp.where(lane == row + 2 * RANK, 1.0, 0.0))
    gram_v[:RANK, :] = eliminate(aug[:RANK], 0)
    gram_v[RANK:, :] = eliminate(aug[RANK:], RANK)
    inv = gram_v[:, 2 * RANK :]

    three = yz_v.at[pl.ds(0, 3)]
    wait_for(three, y_r.at[1])
    ysum_v[my_rows, :] = (yz_v[0] + yz_v[1]) + (yz_v[2] + yz_v[3])
    cp = remote(ysum_v.at[my_rows, :], ysum_v.at[my_rows, :], y_s.at[2], y_r.at[2], partner)
    cp.start()
    cp.wait()

    total = ysum_v[...]
    is_kv = lax.broadcasted_iota(jnp.int32, (RANK, WIDE), 1) < CKV
    both = jnp.concatenate([jnp.where(is_kv, 0.0, total), jnp.where(is_kv, total, 0.0)], axis=0)
    new_t = jnp.dot(inv, both, precision=HIGHEST, preferred_element_type=F32) * (1.0 / 8.0)
    factor = tmm(inv, new_t, precision=HIGHEST)
    bn_o[...] = new_t[:RANK] + new_t[RANK:]
    high, mid = halves(factor)
    stack = jnp.concatenate([high[:RANK], high[:RANK], mid[:RANK], mid[:RANK]], axis=0)
    zq_o[...] = jnp.transpose(stack[:, CKV:COLS])
    zkv_o[...] = jnp.concatenate([high[RANK:], high[RANK:], mid[RANK:], mid[RANK:]], axis=0)[:, :CKV]

    for h in range(PARTS):
        wait_for(rs_buf[h], rs_s.at[h])
        wait_for(zbuf[h].at[pl.ds(0, 3)], zs.at[h])
        wait_for(rs_buf[h], ag_s.at[h])
    wait_for(three, y_s.at[1])


def reduce_call(*args):
    any_spec = pl.BlockSpec(memory_space=pl.ANY)
    vmem_spec = pl.BlockSpec(memory_space=pltpu.VMEM)
    dma = pltpu.SemaphoreType.DMA
    v = pltpu.VMEM
    pair = lambda shape, dtype: [v(tuple(w if n is None else n for n in shape), dtype) for w in WIDTHS]
    outs = [
        *pair((SIDE, CQ, None), BF16),
        *pair((SIDE, CQ, None), BF16),
        *pair((SIDE, None, 2 * CKV), BF16),
        *pair((SIDE, 4 * RANK, None), BF16),
        *pair((SIDE, None, 4 * RANK), BF16),
        v((CQ, 4 * RANK), BF16),
        v((4 * RANK, CKV), BF16),
        v((RANK, WIDE), F32),
    ]
    return pl.pallas_call(
        reduce_kernel,
        out_shape=[jax.ShapeDtypeStruct(o.shape, o.dtype) for o in outs],
        in_specs=[any_spec] * 7,
        out_specs=[vmem_spec] * len(outs),
        scratch_shapes=[
            *pair((SIDE, TOK, None), BF16),
            *[v((CQ, SIDE * w), BF16) for w in WIDTHS],
            *[v((SIDE * w, CKV), BF16) for w in WIDTHS],
            *pair((SIDE, 2 * RANK, None), F32),
            *pair((SIDE, RANK, None), F32),
            *pair((SIDE, RANK, None), F32),
            *pair((SIDE * SIDE - 1, 8, None), F32),
            *pair((SIDE, 8, None), F32),
            *pair((SIDE, 2 * RANK, None), F32),
            v((TOK, CKV), BF16),
            v((COLS, TOK), BF16),
            v((RANK, CQ), F32),
            v((RANK, CKV), F32),
            v((4 * RANK, TOK), BF16),
            v((2 * RANK, CQ), BF16),
            v((2 * RANK, CKV), BF16),
            v((RANK, WIDE), F32),
            v((16, WIDE), F32),
            v((SIDE, 16, WIDE), F32),
            v((RANK, WIDE), F32),
            v((2 * RANK, 128), F32),
            dma((4 + 2 * PARTS,)), dma((SIDE * PARTS,)),
            dma((SIDE * PARTS,)), dma((SIDE * PARTS,)),
            dma((PARTS,)), dma((PARTS,)), dma((PARTS,)), dma((PARTS,)),
            dma((PARTS,)), dma((SIDE * PARTS,)), dma((SIDE * PARTS,)), dma((SIDE * PARTS,)),
            dma((3,)), dma((3,)),
        ],
        compiler_params=pltpu.CompilerParams(collective_id=0, has_side_effects=True, vmem_limit_bytes=40 * MIB),
        name="left_and_right_factors",
    )(*[pltpu.with_memory_space_constraint(a, pltpu.HBM) for a in args])


def write_kernel(*refs):
    parts, refs = by_part(refs, 5)
    zq, zkv, bn, uq, ukv, eq, ekv, bq, bkv, *refs = refs
    staged, (sem,) = by_part(refs, 4)
    copies = []
    for h, (fqh, fqm, fkv, lq, tkv, uq_v, ukv_v, eq_v, ekv_v) in enumerate(zip(*parts, *staged)):
        for g in range(SIDE):
            approx = mm(zq[...], lq[g])
            uq_v[g] = approx.astype(BF16)
            eq_v[g] = (fqh[g].astype(F32) + fqm[g].astype(F32) - approx).astype(BF16)
            approx = mm(tkv[g], zkv[...])
            ukv_v[g] = approx.astype(BF16)
            ekv_v[g] = (fkv[g, :, :CKV].astype(F32) + fkv[g, :, CKV:].astype(F32) - approx).astype(BF16)
            at = pl.ds(STARTS[h] + g * WIDTHS[h], WIDTHS[h])
            pairs = [(uq_v, uq.at[:, at]), (ukv_v, ukv.at[at, :]), (eq_v, eq.at[0, :, at]), (ekv_v, ekv.at[0, at, :])]
            for i, (src, dst) in enumerate(pairs):
                cp = pltpu.make_async_copy(src.at[g], dst, sem.at[h * SIDE + g, i])
                cp.start()
                copies.append(cp)
    bkv[...] = bn[:, :CKV]
    bq[...] = bn[:, CKV:COLS]
    for cp in copies:
        cp.wait()


def write_call(*args):
    vmem_spec = pl.BlockSpec(memory_space=pltpu.VMEM)
    any_spec = pl.BlockSpec(memory_space=pl.ANY)
    pair = lambda *shape: [pltpu.VMEM(tuple(w if n is None else n for n in shape), BF16) for w in WIDTHS]
    return pl.pallas_call(
        write_kernel,
        out_shape=[
            jax.ShapeDtypeStruct((CQ, D), BF16),
            jax.ShapeDtypeStruct((D, CKV), BF16),
            jax.ShapeDtypeStruct((1, CQ, D), BF16),
            jax.ShapeDtypeStruct((1, D, CKV), BF16),
            jax.ShapeDtypeStruct((RANK, CQ), F32),
            jax.ShapeDtypeStruct((RANK, CKV), F32),
        ],
        in_specs=[vmem_spec] * len(args),
        out_specs=[any_spec] * 4 + [vmem_spec] * 2,
        scratch_shapes=[
            *pair(SIDE, CQ, None),
            *pair(SIDE, None, CKV),
            *pair(SIDE, CQ, None),
            *pair(SIDE, None, CKV),
            pltpu.SemaphoreType.DMA((SIDE * PARTS, 4)),
        ],
        compiler_params=pltpu.CompilerParams(vmem_limit_bytes=24 * MIB),
        name="updates_and_errors",
    )(*args)


def local(act, ogq, ogkv, eq, ekv, bq, bkv):
    turned = lambda a: jnp.swapaxes(a, -1, -2)
    got = reduce_call(act, turned(ogq), ogkv, turned(eq), ekv, turned(bq), turned(bkv))
    uq, ukv, eq, ekv, bq, bkv = write_call(*got)
    return (turned(uq), ukv, turned(eq), ekv, turned(bq), turned(bkv))


def solution(mesh):
    placed = (
        P("dp", None, None),
        P("dp", None, "tensor"),
        P("dp", None, "tensor"),
        P("dp", None, "tensor"),
        P("dp", None, "tensor"),
        P("tensor", None),
        P("tensor", None),
    )
    return jax.shard_map(
        local,
        mesh=mesh,
        in_specs=placed,
        out_specs=(
            P(None, "tensor"),
            P(None, "tensor"),
            P("dp", None, "tensor"),
            P("dp", None, "tensor"),
            P("tensor", None),
            P("tensor", None),
        ),
        check_vma=False,
    )
```
